256 devices in a mesh: gx: 32 (over x, y, core), gy: 8 (over z).
Axes of the slice: x: 4, y: 4, z: 8, core: 2. Of those that a mesh axis runs over, the one named last changes fastest.
Arguments:
- pressure: float32 [10, 512, 2048], P(None, 'gx', 'gy'), may hold values from -6 to 6
- conductivity: float32 [10, 512, 2048], P(None, 'gx', 'gy'), may hold values from 0.1 to 10
- storage: float32 [10, 512, 2048], P(None, 'gx', 'gy'), may hold values from 0.5 to 2
- source: float32 [10, 512, 2048], P(None, 'gx', 'gy'), may hold values from -6 to 6
- particles: float32 [32, 8, 104, 8, 128], P('gx', 'gy'), may hold values from 0 to 1
- crossing: int32 [32, 8, 4], P('gx', 'gy'), may hold values from 0 to 16, as said below
- particle_cell: int32 [32, 8, 104, 128], P('gx', 'gy'), may hold values from 0 to 40959
- river_source: int32 [32, 8, 4, 2, 128], P('gx', 'gy'), may hold values from 0 to 4095
- river_target: int32 [32, 8, 4, 2, 128], P('gx', 'gy'), may hold values from 0 to 4095
Outputs:
- pressure_next: float32 [10, 512, 2048], P(None, 'gx', 'gy')
- particles_next: float32 [32, 8, 144, 8, 128], P('gx', 'gy')
- stream_inflow: float32 [512, 2048], P('gx', 'gy')
The draws below stay inside these ranges and needn't reach their ends.
Inputs may be any that keep to these rules, and one draw needn't show every extreme that they name: `crossing`: entries for east and west are at most 16, for north and south at most 4; in every draw some tile sends the most in each direction.
All inputs are finite; a program needn't handle non-finite values.
Results may differ from the reference program's by a relative error of at most 0.0003.
Values sent between devices are 32-bit elements; how exact they have to be, the bound alone decides.
No kernel may reach another device: no remote copies, remote signals or barrier semaphores. Data moves between devices by JAX's collectives and lax.ppermute only.
A program may use at most 64 MiB of HBM per device.

```python
import math
import jax
import jax.numpy as jnp
from jax import lax

CX = 16
CY = 256
NZ = 10
ITERS = 4
ROWS = 128
CAPX = 16
CAPY = 4
RB = 2
PB = 104
NX = 512
NY = 2048
N_GX = 32
N_GY = 8


def draw_crossing(key, part):
    counts_key = jax.random.fold_in(key, 11)
    tile_key = jax.random.fold_in(key, 23)
    upper = jnp.array([CAPX + 1, CAPX + 1, CAPY + 1, CAPY + 1], dtype=jnp.int32)
    values = jax.random.randint(counts_key, (N_GX, N_GY, 4), 0, upper[None, None, :])
    picks = jax.random.randint(tile_key, (2, 4), 0, jnp.array([N_GX, N_GY], dtype=jnp.int32)[:, None])
    rows_x = jnp.arange(N_GX, dtype=jnp.int32)[:, None, None]
    rows_y = jnp.arange(N_GY, dtype=jnp.int32)[None, :, None]
    planted = (rows_x == picks[0][None, None, :]) & (rows_y == picks[1][None, None, :])
    return jnp.where(planted, (upper - 1)[None, None, :], values).astype(jnp.int32)


def plant(result, own_key, low, high):
    shape = result.shape
    index_at = [jax.random.randint(jax.random.fold_in(own_key, axis), (), 0, shape[axis]) for axis in range(len(shape))]
    result = result.at[tuple(index_at)].set(low)
    longest = shape.index(max(shape))
    index_at[longest] = (index_at[longest] + 1) % shape[longest]
    return result.at[tuple(index_at)].set(high)


def block_scale(own_key, extent, cuts, least, top_value):
    def one(axis_at, blocks):
        heights = jax.random.uniform(jax.random.fold_in(jax.random.fold_in(own_key, 6), axis_at), (blocks,), jnp.float32, least / len(cuts), top_value / len(cuts))
        return jnp.repeat(jnp.exp(heights), extent[axis_at] // blocks).reshape((-1,) + (1,) * (len(extent) - axis_at - 1))

    gain = one(*cuts[0])
    for cut in cuts[1:]:
        gain = gain * one(*cut)
    return gain


def centred(own_key, dims, width, reach, shards=(), held_as=jnp.bfloat16):
    entries = width * jax.random.normal(own_key, dims, jnp.float32)
    if shards:
        entries = entries * block_scale(own_key, dims, shards, -0.22, 0.18)
    return jnp.clip(entries, -reach, reach).astype(held_as)


def setup_inputs(seed: int = 0) -> dict:
    keys = jax.random.split(jax.random.key(seed), 10)
    pressure = centred(keys[0], (NZ, NX, NY), 1.0, 6.0, ((1, 32), (2, 8)), jnp.float32)
    conductivity = jnp.clip(jnp.exp(math.log(10.0) - 4.6051702 * jax.random.uniform(keys[1], (NZ, NX, NY), jnp.float32) ** block_scale(keys[1], (NZ, NX, NY), ((1, 32), (2, 8)), -0.2, 0.2)), 0.1, 10.0)
    storage = jnp.clip(jnp.exp(math.log(2.0) - 1.3862944 * jax.random.uniform(keys[2], (NZ, NX, NY), jnp.float32) ** block_scale(keys[2], (NZ, NX, NY), ((1, 32), (2, 8)), -0.2, 0.2)), 0.5, 2.0)
    source = centred(keys[3], (NZ, NX, NY), 1.0, 6.0, ((1, 32), (2, 8)), jnp.float32)
    particles = jnp.clip(1.0 * jax.random.uniform(keys[4], (N_GX, N_GY, PB, 8, ROWS), jnp.float32) ** block_scale(keys[4], (N_GX, N_GY, PB, 8, ROWS), ((0, 32), (1, 8)), -0.2, 0.2), 0.0, 1.0)
    crossing = draw_crossing(jax.random.fold_in(keys[9], 71), 0)
    particle_cell = plant(jax.random.randint(keys[6], (N_GX, N_GY, PB, ROWS), 0, NZ * CX * CY), jax.random.fold_in(keys[6], 1), 0, (NZ * CX * CY) - 1).astype(jnp.int32)
    river_source = plant(jax.random.randint(keys[7], (N_GX, N_GY, 4, RB, ROWS), 0, CX * CY), jax.random.fold_in(keys[7], 1), 0, (CX * CY) - 1).astype(jnp.int32)
    river_target = plant(jax.random.randint(keys[8], (N_GX, N_GY, 4, RB, ROWS), 0, CX * CY), jax.random.fold_in(keys[8], 1), 0, (CX * CY) - 1).astype(jnp.int32)
    return {"pressure": pressure, "conductivity": conductivity, "storage": storage, "source": source, "particles": particles, "crossing": crossing, "particle_cell": particle_cell, "river_source": river_source, "river_target": river_target}


OMEGA_RELAX = 0.8
VERTICAL = 4.0
POROSITY = 0.4
RESIDUAL_SAT = 0.1
TIME_STEP = 0.01
DECAY_RATE = 20.0

def harmonic(left, right):
    total = left + right
    return 2.0 * left * right / (total + (total == 0.0).astype(total.dtype))

def vertical_pair(field):
    zero_layer = jnp.zeros_like(field[:1])
    above = jnp.concatenate([field[1:], zero_layer], 0)
    below = jnp.concatenate([zero_layer, field[:-1]], 0)
    return (above, below)

def jacobi_sweep(press_ext, cond_ext, stor, rhs):
    center = press_ext[:, 1:-1, 1:-1]
    cond_mid = cond_ext[:, 1:-1, 1:-1]
    press_up, press_down = vertical_pair(center)
    cond_up, cond_down = vertical_pair(cond_mid)
    pairs = [(press_ext[:, 2:, 1:-1], cond_ext[:, 2:, 1:-1], 1.0), (press_ext[:, :-2, 1:-1], cond_ext[:, :-2, 1:-1], 1.0), (press_ext[:, 1:-1, 2:], cond_ext[:, 1:-1, 2:], 1.0), (press_ext[:, 1:-1, :-2], cond_ext[:, 1:-1, :-2], 1.0), (press_up, cond_up, VERTICAL), (press_down, cond_down, VERTICAL)]
    applied = stor * center
    diagonal = stor
    for neighbour, cond_near, factor in pairs:
        weight = factor * harmonic(cond_mid, cond_near)
        applied = applied + weight * (center - neighbour)
        diagonal = diagonal + weight
    return center + OMEGA_RELAX * (rhs - applied) / (diagonal + (diagonal == 0.0).astype(diagonal.dtype))

def face_table(press_ext, cond_ext):
    center = press_ext[:, 1:-1, 1:-1]
    cond_mid = cond_ext[:, 1:-1, 1:-1]
    press_up, press_down = vertical_pair(center)
    cond_up, cond_down = vertical_pair(cond_mid)
    east = -harmonic(cond_mid, cond_ext[:, 2:, 1:-1]) * (press_ext[:, 2:, 1:-1] - center)
    west = -harmonic(cond_mid, cond_ext[:, :-2, 1:-1]) * (center - press_ext[:, :-2, 1:-1])
    north = -harmonic(cond_mid, cond_ext[:, 1:-1, 2:]) * (press_ext[:, 1:-1, 2:] - center)
    south = -harmonic(cond_mid, cond_ext[:, 1:-1, :-2]) * (center - press_ext[:, 1:-1, :-2])
    top = -VERTICAL * harmonic(cond_mid, cond_up) * (press_up - center + 1.0)
    bottom = -VERTICAL * harmonic(cond_mid, cond_down) * (center - press_down + 1.0)
    suction = jnp.maximum(-center, 0.0)
    saturation = RESIDUAL_SAT + (1.0 - RESIDUAL_SAT) * lax.rsqrt(1.0 + suction * suction)
    scale = 1.0 / (POROSITY * saturation)
    return jnp.stack([west * scale, east * scale, south * scale, north * scale, bottom * scale, top * scale, saturation])

def advance_records(records, sampled):
    pos_x = records[..., 0, :]
    pos_y = records[..., 1, :]
    pos_z = records[..., 2, :]
    speed_x = sampled[0] + pos_x * (sampled[1] - sampled[0])
    speed_y = sampled[2] + pos_y * (sampled[3] - sampled[2])
    speed_z = sampled[4] + pos_z * (sampled[5] - sampled[4])
    saturation = sampled[6]
    fields = [pos_x + TIME_STEP * speed_x, pos_y + TIME_STEP * speed_y, pos_z + TIME_STEP * speed_z, records[..., 3, :] + TIME_STEP, records[..., 4, :] * jnp.exp(-DECAY_RATE * TIME_STEP * saturation), saturation, records[..., 6, :] + TIME_STEP * speed_x, records[..., 7, :] + TIME_STEP * speed_y]
    return jnp.stack(fields, axis=-2)

def from_lower(array, axis):
    zero = jnp.zeros_like(lax.slice_in_dim(array, 0, 1, axis=axis))
    return jnp.concatenate([zero, lax.slice_in_dim(array, 0, array.shape[axis] - 1, axis=axis)], axis)

def from_upper(array, axis):
    zero = jnp.zeros_like(lax.slice_in_dim(array, 0, 1, axis=axis))
    return jnp.concatenate([lax.slice_in_dim(array, 1, array.shape[axis], axis=axis), zero], axis)

def group_starts():
    return ([0, CAPX, 2 * CAPX, 2 * CAPX + CAPY], [CAPX, CAPX, CAPY, CAPY])

def reference(pressure, conductivity, storage, source, particles, crossing, particle_cell, river_source, river_target):
    margin = ((0, 0), (1, 1), (1, 1))
    rhs = storage * pressure + source
    cond_ext = jnp.pad(conductivity, margin)
    head = pressure
    for sweep_index in range(ITERS):
        head = jacobi_sweep(jnp.pad(head, margin), cond_ext, storage, rhs)
    table = face_table(jnp.pad(head, margin), cond_ext).reshape(7, -1)
    tile_x = jnp.arange(N_GX, dtype=jnp.int32)
    tile_y = jnp.arange(N_GY, dtype=jnp.int32)
    plane = CX * CY
    layer = particle_cell // plane
    within = particle_cell % plane
    glob_x = tile_x[:, None, None, None] * CX + within // CY
    glob_y = tile_y[None, :, None, None] * CY + within % CY
    flat = (layer * NX + glob_x) * NY + glob_y
    sampled = table[:, flat]
    advanced = advance_records(particles, sampled)
    starts, caps = group_starts()
    slot = jnp.arange(PB, dtype=jnp.int32)
    direction = (slot >= starts[1]).astype(jnp.int32) + (slot >= starts[2]).astype(jnp.int32) + (slot >= starts[3]).astype(jnp.int32)
    start_of = jnp.array(starts, dtype=jnp.int32)[direction]
    limit = crossing[:, :, direction]
    live = (slot < 2 * CAPX + 2 * CAPY)[None, None, :] & ((slot - start_of)[None, None, :] < limit)
    kept = jnp.where(live[..., None, None], 0.0, advanced)
    sent = jnp.where(live[..., None, None], advanced, 0.0)

    def outgoing(index):
        return sent[:, :, starts[index]:starts[index] + caps[index]]
    particles_next = jnp.concatenate([kept, from_lower(outgoing(0), 0), from_upper(outgoing(1), 0), from_lower(outgoing(2), 1), from_upper(outgoing(3), 1)], axis=2)
    top_layer = head[NZ - 1]
    src_x = tile_x[:, None, None, None, None] * CX + river_source // CY
    src_y = tile_y[None, :, None, None, None] * CY + river_source % CY
    flow = jax.nn.softplus(top_layer[src_x, src_y])
    arriving = jnp.stack([from_lower(flow[:, :, 0], 0), from_upper(flow[:, :, 1], 0), from_lower(flow[:, :, 2], 1), from_upper(flow[:, :, 3], 1)], axis=2)
    dst_x = tile_x[:, None, None, None, None] * CX + river_target // CY
    dst_y = tile_y[None, :, None, None, None] * CY + river_target % CY
    dst_flat = (dst_x * NY + dst_y).reshape(-1)
    stream_inflow = jnp.zeros((NX * NY,), jnp.float32).at[dst_flat].add(arriving.reshape(-1)).reshape(NX, NY)
    return (head, particles_next, stream_inflow)
```

```python
import functools

import jax
import jax.numpy as jnp
from jax import lax
from jax.experimental import pallas as pl
from jax.experimental.pallas import tpu as pltpu
from jax.sharding import PartitionSpec as P

F32 = jnp.float32
BF16 = jnp.bfloat16

ITERS = 4
CAPX = 16
CAPY = 4
NZ = 10
CX = 16
CY = 256
PB = 104
SENT = 2 * CAPX + 2 * CAPY
KEEP = PB - SENT
OUT = PB + SENT
GROUP = 8

OMEGA_RELAX = 0.8
VERTICAL = 4.0
POROSITY = 0.4
RESIDUAL_SAT = 0.1
TIME_STEP = 0.01
DECAY_RATE = 20.0

ROWS = CX + 8
LANES = CY + 128

EAST = 0
NORTH = 176
SOUTH = 336
LEVEL = 496
SATUR = 640
TABLE = 800


def harmonic(left, right):
    total = left + right
    return 2.0 * left * right / (total + (total == 0.0).astype(total.dtype))


def index_of(shape, axis):
    return lax.broadcasted_iota(jnp.int32, shape, axis)


def roll(x, shift, axis):
    return pltpu.roll(x, shift % x.shape[axis], axis)


def edge_rows_kernel(par_ref, p_ref, c_ref, s_ref, q_ref, even_ref, odd_ref):
    parity = par_ref[0]
    row = index_of((1, 8, CY), 1)
    pieces = []
    for start, step, outer in ((0, -1, 3), (8, 1, 4)):
        tile = slice(start, start + 8)
        p, c, s, q = (ref[:, tile, :] for ref in (p_ref, c_ref, s_ref, q_ref))
        weight = jnp.where(row == outer, harmonic(c, roll(c, step, 1)), 0.0)
        rhs = s * p + q + weight * roll(p, step, 1)
        side = slice(0, 4) if start == 0 else slice(4, 8)
        pieces.append(jnp.concatenate([p[:, side], c[:, side], (s + weight)[:, side], rhs[:, side]], axis=1))
    west, east = pieces
    even_ref[...] = jnp.where(parity == 0, east, west)
    odd_ref[...] = jnp.where(parity == 0, west, east)


def edge_lanes_kernel(par_ref, p_ref, c_ref, s_ref, q_ref, re_ref, ro_ref, ext_ref, even_ref, odd_ref):
    par_x = par_ref[0]
    par_y = par_ref[1]
    own = [p_ref[...], c_ref[...], s_ref[...], s_ref[...] * p_ref[...] + q_ref[...]]
    from_even = re_ref[...]
    from_odd = ro_ref[...]
    east = jnp.where(par_x == 0, from_even, from_odd)
    west = jnp.where(par_x == 0, from_odd, from_even)
    for f in range(4):
        ext_ref[f, :, 0:CX, :] = own[f]
        ext_ref[f, :, CX:ROWS, :] = jnp.concatenate(
            [east[:, 4 * f : 4 * f + 4], west[:, 4 * f : 4 * f + 4]], axis=1
        )
    lane = index_of((1, 1, 128), 2)
    packed = []
    for start, step, outer, low in ((0, -1, 3, 0), (128, 1, 124, 124)):
        p, c, s, r = (ext_ref[f, :, :, start : start + 128] for f in range(4))
        weight = jnp.where(lane == outer, harmonic(c, roll(c, step, 2)), 0.0)
        fields = [p, c, s + weight, r + weight * roll(p, step, 2)]
        inside = (lane >= low) & (lane < low + 4)
        total = [jnp.zeros((8, 128), F32) for _ in range(4)]
        for f in range(4):
            rows = jnp.where(inside, fields[f], 0.0).reshape(30, 8, 128)
            for i in range(30):
                slot = 8 * f + i % 8
                total[i // 8] = total[i // 8] + roll(rows[i], 4 * slot - low, 1)
        packed.append(total)
    south, north = packed
    for j in range(4):
        even_ref[j] = jnp.where(par_y == 0, north[j], south[j])
        odd_ref[j] = jnp.where(par_y == 0, south[j], north[j])


def one_hot(values, size, lanes):
    return jnp.where(index_of((size, lanes), 0) == values, 1.0, 0.0).astype(BF16)


def split(x, parts):
    out = []
    for _ in range(parts):
        piece = x.astype(BF16)
        out.append(piece)
        x = x - piece.astype(F32)
    return out


def sample(tab_ref, cells, found_ref):
    lanes = cells.shape[1]
    hot = one_hot(cells & (CY - 1), CY, lanes)
    found_ref[...] = jnp.dot(tab_ref[...], jnp.concatenate([hot, hot], 0), preferred_element_type=F32)
    high = cells >> 8
    column = high & (CX - 1)
    west_row = jnp.where(column == 0, NZ * CX + (high >> 4), high - 1)
    row = index_of((8, lanes), 0)
    here = high - row
    beside = west_row - row
    west = east = north = south = top = bottom = satur = jnp.zeros((8, lanes), F32)
    for g in range(22):
        at = 8 * g
        face = found_ref[at : at + 8, :]
        west = west + jnp.where(beside == at, face, 0.0)
        if g < 20:
            mask = here == at
            east = east + jnp.where(mask, face, 0.0)
            north = north + jnp.where(mask, found_ref[NORTH + at : NORTH + at + 8, :], 0.0)
            south = south + jnp.where(mask, found_ref[SOUTH + at : SOUTH + at + 8, :], 0.0)
            satur = satur + jnp.where(mask, found_ref[SATUR + at : SATUR + at + 8, :], 0.0)
            if g < 18:
                top = top + jnp.where(mask, found_ref[LEVEL + at : LEVEL + at + 8, :], 0.0)
            if g >= 2:
                bottom = bottom + jnp.where(mask, found_ref[LEVEL + at - 16 : LEVEL + at - 8, :], 0.0)
    return [jnp.sum(v, axis=0, keepdims=True) for v in (west, east, south, north, bottom, top, satur)]


def advance(record, sampled):
    west, east, south, north, bottom, top, satur = sampled
    scale = TIME_STEP / (POROSITY * satur)
    move_x = scale * (west + record[0:1] * (east - west))
    move_y = scale * (south + record[1:2] * (north - south))
    move_z = scale * (bottom + record[2:3] * (top - bottom))
    row = index_of(record.shape, 0)
    step = jnp.where(
        (row == 0) | (row == 6),
        move_x,
        jnp.where((row == 1) | (row == 7), move_y, jnp.where(row == 2, move_z, TIME_STEP)),
    )
    decayed = record * jnp.exp(-DECAY_RATE * TIME_STEP * satur)
    return jnp.where(row == 4, decayed, jnp.where(row == 5, satur, record + step))


def advance_group(tab_ref, cell_ref, rec_ref, found_ref, first, store):
    cells = jnp.concatenate([cell_ref[pl.ds(first + j, 1), :] for j in range(GROUP)], axis=1)
    sampled = sample(tab_ref, cells, found_ref)
    for j in range(GROUP):
        mine = [v[:, 128 * j : 128 * j + 128] for v in sampled]
        store(first + j, advance(rec_ref[first + j], mine))


def sweep_kernel(
    par_ref, cross_ref, ext_ref, re_ref, ro_ref, rec_ref, cell_ref, source_ref,
    head_ref, tab_ref, next_ref, xe_ref, xo_ref, ye_ref, yo_ref,
    h0, h1, cond, rhs, inv, wx, wy, wz, flat, found, kept, sent, sem,
):
    par_x = par_ref[0]
    par_y = par_ref[1]
    lane = index_of((1, 128), 1)
    fields = (h0, cond, inv, rhs)
    north = [jnp.where(par_y == 0, re_ref[j], ro_ref[j]) for j in range(4)]
    south = [jnp.where(par_y == 0, ro_ref[j], re_ref[j]) for j in range(4)]
    for f in range(4):
        for k in range(NZ):
            fields[f][k, :, 0:CY] = ext_ref[f, k]
            for t in range(3):
                i = 3 * k + t
                slot = 8 * f + i % 8
                up = roll(north[i // 8], -4 * slot, 1)
                down = roll(south[i // 8], 124 - 4 * slot, 1)
                fields[f][k, 8 * t : 8 * t + 8, CY:LANES] = jnp.where(
                    lane < 4, up, jnp.where(lane >= 124, down, 0.0)
                )
    row = index_of((ROWS, 1), 0)
    for k in range(NZ):
        c = cond[k]
        w_x = jnp.where(row == CX + 3, 0.0, harmonic(c, roll(c, -1, 0)))
        w_y = harmonic(c, roll(c, -1, 1))
        diag = inv[k] + w_x + roll(w_x, 1, 0) + w_y + roll(w_y, 1, 1)
        if k > 0:
            diag = diag + wz[k - 1]
        if k < NZ - 1:
            w_z = VERTICAL * harmonic(c, cond[k + 1])
            wz[k] = w_z
            diag = diag + w_z
        wx[k] = w_x
        wy[k] = w_y
        inv[k] = OMEGA_RELAX / (diag + (diag == 0.0).astype(F32))
    old, new = h0, h1
    for _ in range(ITERS):
        for k in range(NZ):
            h = old[k]
            w_x = wx[k]
            w_y = wy[k]
            total = rhs[k] + w_x * roll(h, -1, 0) + roll(w_x * h, 1, 0)
            total = total + w_y * roll(h, -1, 1) + roll(w_y * h, 1, 1)
            if k > 0:
                total = total + wz[k - 1] * old[k - 1]
            if k < NZ - 1:
                total = total + wz[k] * old[k + 1]
            new[k] = (1.0 - OMEGA_RELAX) * h + inv[k] * total
        old, new = new, old
    flat[NZ * CX : NORTH, :] = jnp.zeros((16, CY), F32)
    for k in range(NZ):
        h = old[k]
        at = slice(CX * k, CX * k + CX)
        face_x = -wx[k] * (roll(h, -1, 0) - h)
        face_y = -wy[k] * (roll(h, -1, 1) - h)
        mine = h[0:CX, 0:CY]
        head_ref[k] = mine
        flat[EAST + CX * k : EAST + CX * k + CX, :] = face_x[0:CX, 0:CY]
        flat[NZ * CX + k : NZ * CX + k + 1, :] = face_x[ROWS - 1 : ROWS, 0:CY]
        flat[NORTH + CX * k : NORTH + CX * k + CX, :] = face_y[0:CX, 0:CY]
        flat[SOUTH + CX * k : SOUTH + CX * k + CX, :] = roll(face_y, 1, 1)[0:CX, 0:CY]
        if k < NZ - 1:
            face_z = -wz[k, 0:CX, 0:CY] * (old[k + 1, 0:CX, 0:CY] - mine + 1.0)
            flat[LEVEL + CX * k : LEVEL + CX * k + CX, :] = face_z
        suction = jnp.maximum(-mine, 0.0)
        flat[SATUR + CX * k : SATUR + CX * k + CX, :] = RESIDUAL_SAT + (1.0 - RESIDUAL_SAT) * lax.rsqrt(
            1.0 + suction * suction
        )
    coarse, fine = split(flat[...], 2)
    tab_ref[:, 0:CY] = coarse
    tab_ref[:, CY : 2 * CY] = fine

    def store(slot, record):
        group = jnp.where(slot < CAPX, 0, jnp.where(slot < 2 * CAPX, 1, jnp.where(slot < 2 * CAPX + CAPY, 2, 3)))
        start = jnp.where(slot < CAPX, 0, jnp.where(slot < 2 * CAPX, CAPX, jnp.where(slot < 2 * CAPX + CAPY, 2 * CAPX, 2 * CAPX + CAPY)))
        live = slot - start < cross_ref[group]
        kept[slot] = jnp.where(live, 0.0, record)
        sent[slot] = jnp.where(live, record, 0.0)

    def group_step(i, carry):
        advance_group(tab_ref, cell_ref, rec_ref, found, i * GROUP, store)
        return carry

    lax.fori_loop(0, SENT // GROUP, group_step, 0)
    copy = pltpu.make_async_copy(kept, next_ref.at[pl.ds(0, SENT)], sem)
    copy.start()
    links = jnp.concatenate([source_ref[j : j + 1, :] for j in range(8)], axis=1)
    surface = jnp.concatenate(split(old[NZ - 1, 0:CX, 0:CY], 3), axis=0)
    at_links = jnp.dot(surface, one_hot(links & (CY - 1), CY, 1024), preferred_element_type=F32)
    at_links = at_links[0:CX] + at_links[CX : 2 * CX] + at_links[2 * CX : 3 * CX]
    picked = jnp.where(index_of((CX, 1024), 0) == (links >> 8), at_links, 0.0)
    value = jnp.sum(picked, axis=0, keepdims=True)
    flow = jnp.maximum(value, 0.0) + jnp.log1p(jnp.exp(-jnp.abs(value)))
    flows = [
        jnp.concatenate([flow[:, 256 * d : 256 * d + 128], flow[:, 256 * d + 128 : 256 * d + 256]] * 4, axis=0)
        for d in range(4)
    ]
    for ref, par, low, cap in (
        (xe_ref, par_x, 0, CAPX),
        (xo_ref, 1 - par_x, 0, CAPX),
        (ye_ref, par_y, 2, CAPY),
        (yo_ref, 1 - par_y, 2, CAPY),
    ):
        base = 2 * CAPX if low else 0
        ref[0:cap] = sent[pl.ds(base + par * cap, cap)]
        ref[cap] = jnp.where(par == 0, flows[low], flows[low + 1])
    copy.wait()


def rest_kernel(tab_ref, rec_ref, cell_ref, prev_ref, next_ref, found, kept, sem):
    def store(slot, record):
        kept[slot - SENT] = record

    def group_step(i, carry):
        advance_group(tab_ref, cell_ref, rec_ref, found, SENT + i * GROUP, store)
        return carry

    lax.fori_loop(0, KEEP // GROUP, group_step, 0)
    copy = pltpu.make_async_copy(kept, next_ref.at[pl.ds(SENT, KEEP)], sem)
    copy.start()
    copy.wait()


def arrive_kernel(par_ref, target_ref, xe_ref, xo_ref, ye_ref, yo_ref, prev_ref, next_ref, inflow_ref, sems):
    par_x = par_ref[0]
    par_y = par_ref[1]
    copies = []
    for n, (ref, par, base, cap) in enumerate(
        (
            (xe_ref, 1 - par_x, PB, CAPX),
            (xo_ref, par_x, PB, CAPX),
            (ye_ref, 1 - par_y, PB + 2 * CAPX, CAPY),
            (yo_ref, par_y, PB + 2 * CAPX, CAPY),
        )
    ):
        copies.append(
            pltpu.make_async_copy(ref.at[pl.ds(0, cap)], next_ref.at[pl.ds(base + par * cap, cap)], sems.at[n])
        )
    for copy in copies:
        copy.start()
    x_even, x_odd = xe_ref[CAPX], xo_ref[CAPX]
    y_even, y_odd = ye_ref[CAPY], yo_ref[CAPY]
    arrivals = [
        jnp.where(par_x == 0, x_odd, x_even),
        jnp.where(par_x == 0, x_even, x_odd),
        jnp.where(par_y == 0, y_odd, y_even),
        jnp.where(par_y == 0, y_even, y_odd),
    ]
    flow = jnp.concatenate([a[r : r + 1] for a in arrivals for r in range(2)], axis=1)
    links = jnp.concatenate([target_ref[j : j + 1, :] for j in range(8)], axis=1)
    spread = jnp.where(index_of((CX, 1024), 0) == (links >> 8), flow, 0.0)
    parts = jnp.concatenate(split(spread, 3), axis=0)
    hot = one_hot(links & (CY - 1), CY, 1024)
    total = lax.dot_general(parts, hot, (((1,), (1,)), ((), ())), preferred_element_type=F32)
    inflow_ref[...] = total[0:CX] + total[CX : 2 * CX] + total[2 * CX : 3 * CX]
    for copy in copies:
        copy.wait()


VMEM = pl.BlockSpec(memory_space=pltpu.VMEM)
SMEM = pl.BlockSpec(memory_space=pltpu.SMEM)
ANY = pl.BlockSpec(memory_space=pl.ANY)
LIMIT = pltpu.CompilerParams(vmem_limit_bytes=32 << 20)


def swap(size, first):
    pairs = []
    for i in range(first, size - 1, 2):
        pairs += [(i, i + 1), (i + 1, i)]
    return pairs


def exchange(even, odd, axis):
    size = lax.axis_size(axis)
    return lax.ppermute(even, axis, swap(size, 0)), lax.ppermute(odd, axis, swap(size, 1))


def shape(*dims, dtype=F32):
    return jax.ShapeDtypeStruct(dims, dtype)


def body(
    pressure, conductivity, storage, source, particles, crossing, particle_cell, river_source, river_target
):
    parity = jnp.stack([lax.axis_index("gx") % 2, lax.axis_index("gy") % 2]).astype(jnp.int32)
    grid = (pressure, conductivity, storage, source)
    x_even, x_odd = pl.pallas_call(
        edge_rows_kernel,
        out_shape=(shape(NZ, 16, CY), shape(NZ, 16, CY)),
        in_specs=[SMEM] + [VMEM] * 4,
        out_specs=(VMEM, VMEM),
        compiler_params=LIMIT,
        name="edge_rows",
    )(parity, *grid)
    x_even, x_odd = exchange(x_even, x_odd, "gx")
    extended, y_even, y_odd = pl.pallas_call(
        edge_lanes_kernel,
        out_shape=(shape(4, NZ, ROWS, CY), shape(4, 8, 128), shape(4, 8, 128)),
        in_specs=[SMEM] + [VMEM] * 6,
        out_specs=(VMEM,) * 3,
        compiler_params=LIMIT,
        name="edge_lanes",
    )(parity, *grid, x_even, x_odd)
    y_even, y_odd = exchange(y_even, y_odd, "gy")
    records = particles[0, 0]
    cells = particle_cell[0, 0]
    field = pltpu.VMEM((NZ, ROWS, LANES), F32)
    found = pltpu.VMEM((TABLE, 128 * GROUP), F32)
    head, table, moved, x_even, x_odd, y_even, y_odd = pl.pallas_call(
        sweep_kernel,
        out_shape=(
            shape(NZ, CX, CY),
            shape(TABLE, 2 * CY, dtype=BF16),
            shape(OUT, 8, 128),
            shape(CAPX + 1, 8, 128),
            shape(CAPX + 1, 8, 128),
            shape(CAPY + 1, 8, 128),
            shape(CAPY + 1, 8, 128),
        ),
        in_specs=[SMEM, SMEM] + [VMEM] * 6,
        out_specs=(VMEM, VMEM, ANY) + (VMEM,) * 4,
        scratch_shapes=[field] * 8
        + [
            pltpu.VMEM((TABLE, CY), F32),
            found,
            pltpu.VMEM((SENT, 8, 128), F32),
            pltpu.VMEM((SENT, 8, 128), F32),
            pltpu.SemaphoreType.DMA,
        ],
        compiler_params=LIMIT,
        name="sweep",
    )(
        parity, crossing[0, 0], extended, y_even, y_odd, records, cells,
        river_source.reshape(8, 128),
    )
    x_even, x_odd = exchange(x_even, x_odd, "gx")
    y_even, y_odd = exchange(y_even, y_odd, "gy")
    moved = pl.pallas_call(
        rest_kernel,
        out_shape=shape(OUT, 8, 128),
        in_specs=[VMEM] * 3 + [ANY],
        out_specs=ANY,
        scratch_shapes=[found, pltpu.VMEM((KEEP, 8, 128), F32), pltpu.SemaphoreType.DMA],
        input_output_aliases={3: 0},
        compiler_params=LIMIT,
        cost_estimate=pl.CostEstimate(
            flops=2 * TABLE * 512 * 128 * KEEP, bytes_accessed=4 << 20, transcendentals=0
        ),
        name="rest",
    )(table, records, cells, moved)
    moved, inflow = pl.pallas_call(
        arrive_kernel,
        out_shape=(shape(OUT, 8, 128), shape(CX, CY)),
        in_specs=[SMEM] + [VMEM] * 5 + [ANY],
        out_specs=(ANY, VMEM),
        scratch_shapes=[pltpu.SemaphoreType.DMA((4,))],
        input_output_aliases={6: 0},
        compiler_params=LIMIT,
        name="arrive",
    )(parity, river_target.reshape(8, 128), x_even, x_odd, y_even, y_odd, moved)
    return head, moved[None, None], inflow


def solution(mesh):
    in_specs = (
        P(None, "gx", "gy"),
        P(None, "gx", "gy"),
        P(None, "gx", "gy"),
        P(None, "gx", "gy"),
        P("gx", "gy", None, None, None),
        P("gx", "gy", None),
        P("gx", "gy", None, None),
        P("gx", "gy", None, None, None),
        P("gx", "gy", None, None, None),
    )
    out_specs = (P(None, "gx", "gy"), P("gx", "gy", None, None, None), P("gx", "gy"))
    return jax.shard_map(body, mesh=mesh, in_specs=in_specs, out_specs=out_specs, check_vma=False)
```

```python
import functools

import jax
import jax.numpy as jnp
from jax import lax
from jax.experimental import pallas as pl
from jax.experimental.pallas import tpu as pltpu
from jax.sharding import PartitionSpec as P

F32 = jnp.float32
BF16 = jnp.bfloat16

ITERS = 4
CAPX = 16
CAPY = 4
NZ = 10
CX = 16
CY = 256
PB = 104
SENT = 2 * CAPX + 2 * CAPY
KEEP = PB - SENT
OUT = PB + SENT
GROUP_SENT = 20
GROUP_KEEP = 16

OMEGA_RELAX = 0.8
VERTICAL = 4.0
POROSITY = 0.4
RESIDUAL_SAT = 0.1
TIME_STEP = 0.01
DECAY_RATE = 20.0

ROWS = CX + 8
LANES = CY + 128

EAST = 0
NORTH = 176
SOUTH = 336
LEVEL = 496
SATUR = 640
TABLE = 800


def harmonic(left, right):
    total = left + right
    return 2.0 * left * right / (total + (total == 0.0).astype(total.dtype))


def index_of(shape, axis):
    return lax.broadcasted_iota(jnp.int32, shape, axis)


def roll(x, shift, axis):
    return pltpu.roll(x, shift % x.shape[axis], axis)


def parities():
    return lax.rem(lax.axis_index("gx"), 2), lax.rem(lax.axis_index("gy"), 2)


def edge_rows_kernel(p_hbm, c_hbm, s_hbm, q_hbm, even_hbm, odd_hbm, p_ref, c_ref, s_ref, q_ref, even_ref, odd_ref, sems):
    halves = (slice(0, NZ // 2), slice(NZ // 2, NZ))
    loads = []
    for h, part in enumerate(halves):
        pairs = ((p_hbm, p_ref), (c_hbm, c_ref), (s_hbm, s_ref), (q_hbm, q_ref))
        loads.append([pltpu.make_async_copy(a.at[part], b.at[part], sems.at[h, n]) for n, (a, b) in enumerate(pairs)])
        for copy in loads[h]:
            copy.start()
    parity = parities()[0]
    row = index_of((1, 8, CY), 1)
    stores = []
    for h, part in enumerate(halves):
        for copy in loads[h]:
            copy.wait()
        pieces = []
        for start, step, outer in ((0, -1, 3), (8, 1, 4)):
            tile = slice(start, start + 8)
            p, c, s, q = (ref[part, tile, :] for ref in (p_ref, c_ref, s_ref, q_ref))
            weight = jnp.where(row == outer, harmonic(c, roll(c, step, 1)), 0.0)
            rhs = s * p + q + weight * roll(p, step, 1)
            side = slice(0, 4) if start == 0 else slice(4, 8)
            pieces.append(jnp.concatenate([p[:, side], c[:, side], (s + weight)[:, side], rhs[:, side]], axis=1))
        west, east = pieces
        even_ref[part] = jnp.where(parity == 0, east, west)
        odd_ref[part] = jnp.where(parity == 0, west, east)
        for n, (a, b) in enumerate(((even_ref, even_hbm), (odd_ref, odd_hbm))):
            copy = pltpu.make_async_copy(a.at[part], b.at[part], sems.at[h, 4 + n])
            copy.start()
            stores.append(copy)
    for copy in stores:
        copy.wait()


def beside_rows(from_even, from_odd, par_x):
    east = jnp.where(par_x == 0, from_even, from_odd)
    west = jnp.where(par_x == 0, from_odd, from_even)
    return [jnp.concatenate([east[:, 4 * f : 4 * f + 4], west[:, 4 * f : 4 * f + 4]], axis=1) for f in range(4)]


def edge_lanes_kernel(p_ref, c_ref, s_ref, q_ref, re_ref, ro_ref, links_ref, cross_ref, even_ref, odd_ref):
    par_x, par_y = parities()
    lane = index_of((1, 1, 128), 2)
    packed = []
    for start, step, outer, low in ((0, -1, 3, 0), (128, 1, 124, 124)):
        at = slice(start, start + 128)
        near = beside_rows(re_ref[:, :, at], ro_ref[:, :, at], par_x)
        p, c, s, q = (ref[:, :, at] for ref in (p_ref, c_ref, s_ref, q_ref))
        p, c, s, r = (jnp.concatenate(pair, axis=1) for pair in zip((p, c, s, s * p + q), near))
        weight = jnp.where(lane == outer, harmonic(c, roll(c, step, 2)), 0.0)
        fields = [p, c, s + weight, r + weight * roll(p, step, 2)]
        inside = (lane >= low) & (lane < low + 4)
        total = [jnp.zeros((8, 128), F32) for _ in range(4)]
        for f in range(4):
            rows = jnp.where(inside, fields[f], 0.0).reshape(30, 8, 128)
            for i in range(30):
                slot = 8 * f + i % 8
                total[i // 8] = total[i // 8] + roll(rows[i], 4 * slot - low, 1)
        packed.append(total)
    south, north = packed
    for j in range(4):
        even_ref[j] = jnp.where(par_y == 0, north[j], south[j])
        odd_ref[j] = jnp.where(par_y == 0, south[j], north[j])


def one_hot(values, lanes):
    hit = index_of((CY, lanes), 0).astype(BF16) == values.astype(BF16)
    return jnp.where(hit, jnp.ones((), BF16), jnp.zeros((), BF16))


def split(x, parts):
    out = []
    for _ in range(parts):
        piece = x.astype(BF16)
        out.append(piece)
        x = x - piece.astype(F32)
    return out


def sample(tab_ref, cells, found_ref):
    lanes = cells.shape[1]
    hot = one_hot(cells & (CY - 1), lanes)
    found_ref[...] = jnp.dot(tab_ref[...], jnp.concatenate([hot, hot], 0), preferred_element_type=F32)
    high = cells >> 8
    column = high & (CX - 1)
    west_row = jnp.where(column == 0, NZ * CX + (high >> 4), high - 1)
    here = jnp.broadcast_to(high >> 3, (8, lanes))
    beside = jnp.broadcast_to(west_row >> 3, (8, lanes))
    west = east = north = south = top = bottom = satur = jnp.zeros((8, lanes), F32)
    for g in range(22):
        at = 8 * g
        face = found_ref[at : at + 8, :]
        west = jnp.where(beside == g, face, west)
        if g < 20:
            mask = here == g
            east = jnp.where(mask, face, east)
            north = jnp.where(mask, found_ref[NORTH + at : NORTH + at + 8, :], north)
            south = jnp.where(mask, found_ref[SOUTH + at : SOUTH + at + 8, :], south)
            satur = jnp.where(mask, found_ref[SATUR + at : SATUR + at + 8, :], satur)
            if g < 18:
                top = jnp.where(mask, found_ref[LEVEL + at : LEVEL + at + 8, :], top)
            if g >= 2:
                bottom = jnp.where(mask, found_ref[LEVEL + at - 16 : LEVEL + at - 8, :], bottom)
    row = index_of((8, lanes), 0)
    own = row == (high & 7)
    other = row == (west_row & 7)

    def pick(mask, rows):
        return jnp.sum(jnp.where(mask, rows, 0.0), axis=0, keepdims=True)

    return [pick(other, west)] + [pick(own, v) for v in (east, south, north, bottom, top, satur)]


def advance(record, sampled):
    west, east, south, north, bottom, top, satur = sampled
    scale = TIME_STEP / (POROSITY * satur)
    move_x = scale * (west + record[0:1] * (east - west))
    move_y = scale * (south + record[1:2] * (north - south))
    move_z = scale * (bottom + record[2:3] * (top - bottom))
    row = index_of(record.shape, 0)
    step = jnp.where(
        (row == 0) | (row == 6),
        move_x,
        jnp.where((row == 1) | (row == 7), move_y, jnp.where(row == 2, move_z, TIME_STEP)),
    )
    decayed = record * jnp.exp(-DECAY_RATE * TIME_STEP * satur)
    return jnp.where(row == 4, decayed, jnp.where(row == 5, satur, record + step))


def advance_group(tab_ref, cell_ref, rec_ref, found_ref, first, size, store):
    cells = jnp.concatenate([cell_ref[pl.ds(first + j, 1), :] for j in range(size)], axis=1)
    sampled = sample(tab_ref, cells, found_ref)
    for j in range(size):
        mine = [v[:, 128 * j : 128 * j + 128] for v in sampled]
        store(first + j, advance(rec_ref[first + j], mine))


def sweep_kernel(
    cross_ref, p_ref, c_ref, s_ref, q_ref, rxe_ref, rxo_ref, rye_ref, ryo_ref, rec_ref, cell_ref, source_ref,
    head_ref, tab_ref, next_ref, xe_ref, xo_ref, ye_ref, yo_ref,
    h0, h1, cond, rhs, inv, wx, wy, wz, flat, found, kept, sent, final, sems,
):
    par_x, par_y = parities()
    lane = index_of((1, 128), 1)
    fields = (h0, cond, inv, rhs)
    near = beside_rows(rxe_ref[...], rxo_ref[...], par_x)
    h0[:, 0:CX, 0:CY] = p_ref[...]
    cond[:, 0:CX, 0:CY] = c_ref[...]
    inv[:, 0:CX, 0:CY] = s_ref[...]
    rhs[:, 0:CX, 0:CY] = s_ref[...] * p_ref[...] + q_ref[...]
    north = [jnp.where(par_y == 0, rye_ref[j], ryo_ref[j]) for j in range(4)]
    south = [jnp.where(par_y == 0, ryo_ref[j], rye_ref[j]) for j in range(4)]
    for f in range(4):
        fields[f][:, CX:ROWS, 0:CY] = near[f]
        for i in range(30):
            slot = 8 * f + i % 8
            up = roll(north[i // 8], -4 * slot, 1)
            down = roll(south[i // 8], 124 - 4 * slot, 1)
            fields[f][i // 3, 8 * (i % 3) : 8 * (i % 3) + 8, CY:LANES] = jnp.where(
                lane < 4, up, jnp.where(lane >= 124, down, 0.0)
            )
    row = index_of((ROWS, 1), 0)
    for k in range(NZ):
        c = cond[k]
        w_x = jnp.where(row == CX + 3, 0.0, harmonic(c, roll(c, -1, 0)))
        w_y = harmonic(c, roll(c, -1, 1))
        diag = inv[k] + w_x + roll(w_x, 1, 0) + w_y + roll(w_y, 1, 1)
        if k > 0:
            diag = diag + wz[k - 1]
        if k < NZ - 1:
            w_z = VERTICAL * harmonic(c, cond[k + 1])
            wz[k] = w_z
            diag = diag + w_z
        wx[k] = w_x
        wy[k] = w_y
        inv[k] = OMEGA_RELAX / (diag + (diag == 0.0).astype(F32))
    old, new = h0, h1
    for _ in range(ITERS):
        for k in range(NZ):
            h = old[k]
            w_x = wx[k]
            w_y = wy[k]
            total = rhs[k] + w_x * roll(h, -1, 0) + roll(w_x * h, 1, 0)
            total = total + w_y * roll(h, -1, 1) + roll(w_y * h, 1, 1)
            if k > 0:
                total = total + wz[k - 1] * old[k - 1]
            if k < NZ - 1:
                total = total + wz[k] * old[k + 1]
            new[k] = (1.0 - OMEGA_RELAX) * h + inv[k] * total
        old, new = new, old
    flat[NZ * CX : NORTH, :] = jnp.zeros((16, CY), F32)
    for k in range(NZ):
        h = old[k]
        at = slice(CX * k, CX * k + CX)
        face_x = -wx[k] * (roll(h, -1, 0) - h)
        face_y = -wy[k] * (roll(h, -1, 1) - h)
        mine = h[0:CX, 0:CY]
        final[k] = mine
        flat[EAST + CX * k : EAST + CX * k + CX, :] = face_x[0:CX, 0:CY]
        flat[NZ * CX + k : NZ * CX + k + 1, :] = face_x[ROWS - 1 : ROWS, 0:CY]
        flat[NORTH + CX * k : NORTH + CX * k + CX, :] = face_y[0:CX, 0:CY]
        flat[SOUTH + CX * k : SOUTH + CX * k + CX, :] = roll(face_y, 1, 1)[0:CX, 0:CY]
        if k < NZ - 1:
            face_z = -wz[k, 0:CX, 0:CY] * (old[k + 1, 0:CX, 0:CY] - mine + 1.0)
            flat[LEVEL + CX * k : LEVEL + CX * k + CX, :] = face_z
        suction = jnp.maximum(-mine, 0.0)
        flat[SATUR + CX * k : SATUR + CX * k + CX, :] = RESIDUAL_SAT + (1.0 - RESIDUAL_SAT) * lax.rsqrt(
            1.0 + suction * suction
        )
    head_copy = pltpu.make_async_copy(final, head_ref, sems.at[0])
    head_copy.start()
    coarse, fine = split(flat[...], 2)
    tab_ref[:, 0:CY] = coarse
    tab_ref[:, CY : 2 * CY] = fine

    def store(slot, record):
        group = jnp.where(slot < CAPX, 0, jnp.where(slot < 2 * CAPX, 1, jnp.where(slot < 2 * CAPX + CAPY, 2, 3)))
        start = jnp.where(slot < CAPX, 0, jnp.where(slot < 2 * CAPX, CAPX, jnp.where(slot < 2 * CAPX + CAPY, 2 * CAPX, 2 * CAPX + CAPY)))
        live = slot - start < cross_ref[group]
        kept[slot] = jnp.where(live, 0.0, record)
        sent[slot] = jnp.where(live, record, 0.0)

    def group_step(i, carry):
        advance_group(tab_ref, cell_ref, rec_ref, found, i * GROUP_SENT, GROUP_SENT, store)
        return carry

    lax.fori_loop(0, SENT // GROUP_SENT, group_step, 0)
    copy = pltpu.make_async_copy(kept, next_ref.at[pl.ds(0, SENT)], sems.at[1])
    copy.start()
    links = jnp.concatenate([source_ref[j : j + 1, :] for j in range(8)], axis=1)
    surface = jnp.concatenate(split(old[NZ - 1, 0:CX, 0:CY], 3), axis=0)
    at_links = jnp.dot(surface, one_hot(links & (CY - 1), 1024), preferred_element_type=F32)
    at_links = at_links[0:CX] + at_links[CX : 2 * CX] + at_links[2 * CX : 3 * CX]
    picked = jnp.where(index_of((CX, 1024), 0) == (links >> 8), at_links, 0.0)
    value = jnp.sum(picked, axis=0, keepdims=True)
    flow = jnp.maximum(value, 0.0) + jnp.log1p(jnp.exp(-jnp.abs(value)))
    flows = [
        jnp.concatenate([flow[:, 256 * d : 256 * d + 128], flow[:, 256 * d + 128 : 256 * d + 256]] * 4, axis=0)
        for d in range(4)
    ]
    for ref, par, low, cap in (
        (xe_ref, par_x, 0, CAPX),
        (xo_ref, 1 - par_x, 0, CAPX),
        (ye_ref, par_y, 2, CAPY),
        (yo_ref, 1 - par_y, 2, CAPY),
    ):
        base = 2 * CAPX if low else 0
        ref[0:cap] = sent[pl.ds(base + par * cap, cap)]
        ref[cap] = jnp.where(par == 0, flows[low], flows[low + 1])
    copy.wait()
    head_copy.wait()


def rest_kernel(tab_ref, rec_ref, cell_ref, prev_ref, next_ref, found, kept, sem):
    def store(slot, record):
        kept[slot - SENT] = record

    def group_step(i, carry):
        advance_group(tab_ref, cell_ref, rec_ref, found, SENT + i * GROUP_KEEP, GROUP_KEEP, store)
        return carry

    lax.fori_loop(0, KEEP // GROUP_KEEP, group_step, 0)
    copy = pltpu.make_async_copy(kept, next_ref.at[pl.ds(SENT, KEEP)], sem)
    copy.start()
    copy.wait()


def arrive_kernel(target_ref, xe_ref, xo_ref, ye_ref, yo_ref, prev_ref, next_ref, inflow_ref, sems):
    par_x, par_y = parities()
    copies = []
    for n, (ref, par, base, cap) in enumerate(
        (
            (xe_ref, 1 - par_x, PB, CAPX),
            (xo_ref, par_x, PB, CAPX),
            (ye_ref, 1 - par_y, PB + 2 * CAPX, CAPY),
            (yo_ref, par_y, PB + 2 * CAPX, CAPY),
        )
    ):
        copies.append(
            pltpu.make_async_copy(ref.at[pl.ds(0, cap)], next_ref.at[pl.ds(base + par * cap, cap)], sems.at[n])
        )
    for copy in copies:
        copy.start()
    x_even, x_odd = xe_ref[CAPX], xo_ref[CAPX]
    y_even, y_odd = ye_ref[CAPY], yo_ref[CAPY]
    arrivals = [
        jnp.where(par_x == 0, x_odd, x_even),
        jnp.where(par_x == 0, x_even, x_odd),
        jnp.where(par_y == 0, y_odd, y_even),
        jnp.where(par_y == 0, y_even, y_odd),
    ]
    flow = jnp.concatenate([a[r : r + 1] for a in arrivals for r in range(2)], axis=1)
    links = jnp.concatenate([target_ref[j : j + 1, :] for j in range(8)], axis=1)
    spread = jnp.where(index_of((CX, 1024), 0) == (links >> 8), flow, 0.0)
    parts = jnp.concatenate(split(spread, 3), axis=0)
    hot = one_hot(links & (CY - 1), 1024)
    total = lax.dot_general(parts, hot, (((1,), (1,)), ((), ())), preferred_element_type=F32)
    inflow_ref[...] = total[0:CX] + total[CX : 2 * CX] + total[2 * CX : 3 * CX]
    for copy in copies:
        copy.wait()


VMEM = pl.BlockSpec(memory_space=pltpu.VMEM)
SMEM = pl.BlockSpec(memory_space=pltpu.SMEM)
ANY = pl.BlockSpec(memory_space=pl.ANY)
LIMIT = pltpu.CompilerParams(vmem_limit_bytes=32 << 20)


def swap(size, first):
    pairs = []
    for i in range(first, size - 1, 2):
        pairs += [(i, i + 1), (i + 1, i)]
    return pairs


def exchange(even, odd, axis):
    size = lax.axis_size(axis)
    from_odd = lax.ppermute(odd, axis, swap(size, 1))
    from_even = lax.ppermute(even, axis, swap(size, 0))
    return from_even, from_odd


def shape(*dims, dtype=F32):
    return jax.ShapeDtypeStruct(dims, dtype)


def body(
    pressure, conductivity, storage, source, particles, crossing, particle_cell, river_source, river_target
):
    links = river_source.reshape(8, 128)
    grid = (pressure, conductivity, storage, source)
    tile = pltpu.VMEM((NZ, CX, CY), F32)
    x_even, x_odd = pl.pallas_call(
        edge_rows_kernel,
        out_shape=(shape(NZ, CX, CY), shape(NZ, CX, CY)),
        in_specs=[ANY] * 4,
        out_specs=(ANY, ANY),
        scratch_shapes=[tile] * 6 + [pltpu.SemaphoreType.DMA((2, 6))],
        compiler_params=pltpu.CompilerParams(vmem_limit_bytes=60 << 20),
        name="edge_rows",
    )(*grid)
    halo_x = exchange(x_even, x_odd, "gx")
    y_even, y_odd = pl.pallas_call(
        edge_lanes_kernel,
        out_shape=(shape(4, 8, 128), shape(4, 8, 128)),
        in_specs=[VMEM] * 7 + [SMEM],
        out_specs=(VMEM, VMEM),
        compiler_params=LIMIT,
        name="edge_lanes",
    )(*grid, *halo_x, links, crossing[0, 0])
    halo_y = exchange(y_even, y_odd, "gy")
    records = particles[0, 0]
    cells = particle_cell[0, 0]
    field = pltpu.VMEM((NZ, ROWS, LANES), F32)
    head, table, moved, x_even, x_odd, y_even, y_odd = pl.pallas_call(
        sweep_kernel,
        out_shape=(
            shape(NZ, CX, CY),
            shape(TABLE, 2 * CY, dtype=BF16),
            shape(OUT, 8, 128),
            shape(CAPX + 1, 8, 128),
            shape(CAPX + 1, 8, 128),
            shape(CAPY + 1, 8, 128),
            shape(CAPY + 1, 8, 128),
        ),
        in_specs=[SMEM] + [VMEM] * 11,
        out_specs=(ANY, VMEM, ANY) + (VMEM,) * 4,
        scratch_shapes=[field] * 8
        + [
            pltpu.VMEM((TABLE, CY), F32),
            pltpu.VMEM((TABLE, 128 * GROUP_SENT), F32),
            pltpu.VMEM((SENT, 8, 128), F32),
            pltpu.VMEM((SENT, 8, 128), F32),
            tile,
            pltpu.SemaphoreType.DMA((2,)),
        ],
        compiler_params=LIMIT,
        name="sweep",
    )(crossing[0, 0], *grid, *halo_x, *halo_y, records, cells, links)
    x_even, x_odd = exchange(x_even, x_odd, "gx")
    y_even, y_odd = exchange(y_even, y_odd, "gy")
    moved = pl.pallas_call(
        rest_kernel,
        out_shape=shape(OUT, 8, 128),
        in_specs=[VMEM] * 3 + [ANY],
        out_specs=ANY,
        scratch_shapes=[pltpu.VMEM((TABLE, 128 * GROUP_KEEP), F32), pltpu.VMEM((KEEP, 8, 128), F32), pltpu.SemaphoreType.DMA],
        input_output_aliases={3: 0},
        compiler_params=LIMIT,
        cost_estimate=pl.CostEstimate(
            flops=2 * TABLE * 512 * 128 * KEEP, bytes_accessed=4 << 20, transcendentals=0
        ),
        name="rest",
    )(table, records, cells, moved)
    moved, inflow = pl.pallas_call(
        arrive_kernel,
        out_shape=(shape(OUT, 8, 128), shape(CX, CY)),
        in_specs=[VMEM] * 5 + [ANY],
        out_specs=(ANY, VMEM),
        scratch_shapes=[pltpu.SemaphoreType.DMA((4,))],
        input_output_aliases={5: 0},
        compiler_params=LIMIT,
        name="arrive",
    )(river_target.reshape(8, 128), x_even, x_odd, y_even, y_odd, moved)
    return head, moved[None, None], inflow


def solution(mesh):
    in_specs = (
        P(None, "gx", "gy"),
        P(None, "gx", "gy"),
        P(None, "gx", "gy"),
        P(None, "gx", "gy"),
        P("gx", "gy", None, None, None),
        P("gx", "gy", None),
        P("gx", "gy", None, None),
        P("gx", "gy", None, None, None),
        P("gx", "gy", None, None, None),
    )
    out_specs = (P(None, "gx", "gy"), P("gx", "gy", None, None, None), P("gx", "gy"))
    return jax.shard_map(body, mesh=mesh, in_specs=in_specs, out_specs=out_specs, check_vma=False)
```

```python
import functools

import jax
import jax.numpy as jnp
from jax import lax
from jax.experimental import pallas as pl
from jax.experimental.pallas import tpu as pltpu
from jax.sharding import PartitionSpec as P

F32 = jnp.float32
BF16 = jnp.bfloat16

ITERS = 4
CAPX = 16
CAPY = 4
NZ = 10
CX = 16
CY = 256
PB = 104
SENT = 2 * CAPX + 2 * CAPY
KEEP = PB - SENT
OUT = PB + SENT
GROUP_SENT = 20
GROUP_KEEP = 16

OMEGA_RELAX = 0.8
VERTICAL = 4.0
POROSITY = 0.4
RESIDUAL_SAT = 0.1
TIME_STEP = 0.01
DECAY_RATE = 20.0

ROWS = CX + 8
TALL = 8 + ROWS + 8
MID = slice(8, 8 + ROWS)
OWN = slice(12, 12 + CX)
INNER = slice(4, 4 + CX)

EAST = 0
NORTH = 176
SOUTH = 336
LEVEL = 496
SATUR = 640
TABLE = 800


def harmonic(left, right):
    total = left + right
    return 2.0 * left * right / (total + (total == 0.0).astype(total.dtype))


def index_of(shape, axis):
    return lax.broadcasted_iota(jnp.int32, shape, axis)


def roll(x, shift, axis):
    return pltpu.roll(x, shift % x.shape[axis], axis)


def parities():
    return lax.rem(lax.axis_index("gx"), 2), lax.rem(lax.axis_index("gy"), 2)


def edge_rows_kernel(p_hbm, c_hbm, s_hbm, q_hbm, even_hbm, odd_hbm, p_ref, c_ref, s_ref, q_ref, even_ref, odd_ref, sems):
    halves = (slice(0, NZ // 2), slice(NZ // 2, NZ))
    loads = []
    for h, part in enumerate(halves):
        pairs = ((p_hbm, p_ref), (c_hbm, c_ref), (s_hbm, s_ref), (q_hbm, q_ref))
        loads.append([pltpu.make_async_copy(a.at[part], b.at[part], sems.at[h, n]) for n, (a, b) in enumerate(pairs)])
        for copy in loads[h]:
            copy.start()
    parity = parities()[0]
    row = index_of((1, 8, CY), 1)
    stores = []
    for h, part in enumerate(halves):
        for copy in loads[h]:
            copy.wait()
        pieces = []
        for start, step, outer in ((0, -1, 3), (8, 1, 4)):
            tile = slice(start, start + 8)
            p, c, s, q = (ref[part, tile, :] for ref in (p_ref, c_ref, s_ref, q_ref))
            weight = jnp.where(row == outer, harmonic(c, roll(c, step, 1)), 0.0)
            rhs = s * p + q + weight * roll(p, step, 1)
            side = slice(0, 4) if start == 0 else slice(4, 8)
            pieces.append(jnp.concatenate([p[:, side], c[:, side], (s + weight)[:, side], rhs[:, side]], axis=1))
        west, east = pieces
        even_ref[part] = jnp.where(parity == 0, east, west)
        odd_ref[part] = jnp.where(parity == 0, west, east)
        for n, (a, b) in enumerate(((even_ref, even_hbm), (odd_ref, odd_hbm))):
            copy = pltpu.make_async_copy(a.at[part], b.at[part], sems.at[h, 4 + n])
            copy.start()
            stores.append(copy)
    for copy in stores:
        copy.wait()


def beside_rows(from_even, from_odd, par_x):
    east = jnp.where(par_x == 0, from_even, from_odd)
    west = jnp.where(par_x == 0, from_odd, from_even)
    return [jnp.concatenate([east[:, 4 * f : 4 * f + 4], west[:, 4 * f : 4 * f + 4]], axis=1) for f in range(4)]


def edge_lanes_kernel(p_ref, c_ref, s_ref, q_ref, re_ref, ro_ref, even_ref, odd_ref):
    par_x, par_y = parities()
    lane = index_of((1, 1, 128), 2)
    packed = []
    for start, step, outer, low in ((0, -1, 3, 0), (128, 1, 124, 124)):
        at = slice(start, start + 128)
        near = beside_rows(re_ref[:, :, at], ro_ref[:, :, at], par_x)
        p, c, s, q = (ref[:, :, at] for ref in (p_ref, c_ref, s_ref, q_ref))
        p, c, s, r = (jnp.concatenate(pair, axis=1) for pair in zip((p, c, s, s * p + q), near))
        weight = jnp.where(lane == outer, harmonic(c, roll(c, step, 2)), 0.0)
        fields = [p, c, s + weight, r + weight * roll(p, step, 2)]
        inside = (lane >= low) & (lane < low + 4)
        total = [jnp.zeros((8, 128), F32) for _ in range(4)]
        for f in range(4):
            rows = jnp.where(inside, fields[f], 0.0).reshape(30, 8, 128)
            for i in range(30):
                slot = 8 * f + i % 8
                total[i // 8] = total[i // 8] + roll(rows[i], 4 * slot - low, 1)
        packed.append(total)
    south, north = packed
    for j in range(4):
        even_ref[j] = jnp.where(par_y == 0, north[j], south[j])
        odd_ref[j] = jnp.where(par_y == 0, south[j], north[j])


def one_hot(values, lanes):
    hit = index_of((CY, lanes), 0).astype(BF16) == values.astype(BF16)
    return jnp.where(hit, jnp.ones((), BF16), jnp.zeros((), BF16))


def split(x, parts):
    out = []
    for _ in range(parts):
        piece = x.astype(BF16)
        out.append(piece)
        x = x - piece.astype(F32)
    return out


def sample(tab_ref, cells, found_ref):
    lanes = cells.shape[1]
    hot = one_hot(cells & (CY - 1), lanes)
    found_ref[...] = jnp.dot(tab_ref[...], jnp.concatenate([hot, hot], 0), preferred_element_type=F32)
    high = cells >> 8
    column = high & (CX - 1)
    west_row = jnp.where(column == 0, NZ * CX + (high >> 4), high - 1)
    here = jnp.broadcast_to(high >> 3, (8, lanes))
    beside = jnp.broadcast_to(west_row >> 3, (8, lanes))
    west = east = north = south = top = bottom = satur = jnp.zeros((8, lanes), F32)
    for g in range(22):
        at = 8 * g
        face = found_ref[at : at + 8, :]
        west = jnp.where(beside == g, face, west)
        if g < 20:
            mask = here == g
            east = jnp.where(mask, face, east)
            north = jnp.where(mask, found_ref[NORTH + at : NORTH + at + 8, :], north)
            south = jnp.where(mask, found_ref[SOUTH + at : SOUTH + at + 8, :], south)
            satur = jnp.where(mask, found_ref[SATUR + at : SATUR + at + 8, :], satur)
            if g < 18:
                top = jnp.where(mask, found_ref[LEVEL + at : LEVEL + at + 8, :], top)
            if g >= 2:
                bottom = jnp.where(mask, found_ref[LEVEL + at - 16 : LEVEL + at - 8, :], bottom)
    row = index_of((8, lanes), 0)
    own = row == (high & 7)
    other = row == (west_row & 7)

    def pick(mask, rows):
        return jnp.sum(jnp.where(mask, rows, 0.0), axis=0, keepdims=True)

    return [pick(other, west)] + [pick(own, v) for v in (east, south, north, bottom, top, satur)]


def advance(record, sampled):
    west, east, south, north, bottom, top, satur = sampled
    scale = TIME_STEP / (POROSITY * satur)
    move_x = scale * (west + record[0:1] * (east - west))
    move_y = scale * (south + record[1:2] * (north - south))
    move_z = scale * (bottom + record[2:3] * (top - bottom))
    row = index_of(record.shape, 0)
    step = jnp.where(
        (row == 0) | (row == 6),
        move_x,
        jnp.where((row == 1) | (row == 7), move_y, jnp.where(row == 2, move_z, TIME_STEP)),
    )
    decayed = record * jnp.exp(-DECAY_RATE * TIME_STEP * satur)
    return jnp.where(row == 4, decayed, jnp.where(row == 5, satur, record + step))


def advance_group(tab_ref, cell_ref, rec_ref, found_ref, first, size, store):
    cells = jnp.concatenate([cell_ref[pl.ds(first + j, 1), :] for j in range(size)], axis=1)
    sampled = sample(tab_ref, cells, found_ref)
    for j in range(size):
        mine = [v[:, 128 * j : 128 * j + 128] for v in sampled]
        store(first + j, advance(rec_ref[first + j], mine))


def beside_lanes(tiles):
    lane = index_of(tiles[0].shape, 1)
    ahead = [roll(t, -1, 1) for t in tiles]
    back = [roll(t, 1, 1) for t in tiles]
    after = [jnp.where(lane == 127, ahead[(j + 1) % 3], ahead[j]) for j in range(3)]
    before = [jnp.where(lane == 0, back[(j + 2) % 3], back[j]) for j in range(3)]
    return after, before


def sweep_kernel(
    small_ref, p_ref, c_ref, s_ref, q_ref, rxe_ref, rxo_ref, rye_ref, ryo_ref, rec_ref, cell_ref,
    head_ref, tab_ref, next_ref, xe_ref, xo_ref, ye_ref, yo_ref,
    h0, h1, cond, wx, rhs, inv, wy, wy_back, wz, flat, found, kept, sent, final, live_ref, sems,
):
    par_x, par_y = parities()
    edge = jnp.zeros((NZ, 3, 8, 128), F32)
    for ref in (h0, h1, cond, wx):
        ref[:, :, 0:8, :] = edge
        ref[:, :, 8 + ROWS : TALL, :] = edge
    east = jnp.where(par_x == 0, rxe_ref[...], rxo_ref[...])
    west = jnp.where(par_x == 0, rxo_ref[...], rxe_ref[...])
    north = [jnp.where(par_y == 0, rye_ref[j], ryo_ref[j]) for j in range(4)]
    south = [jnp.where(par_y == 0, ryo_ref[j], rye_ref[j]) for j in range(4)]
    lane = index_of((1, 128), 1)
    for f, (ref, base) in enumerate(((h0, 8), (cond, 8), (inv, 0), (rhs, 0))):
        for j in range(2):
            at = slice(128 * j, 128 * j + 128)
            own = (p_ref, c_ref, s_ref)[f][:, :, at] if f < 3 else s_ref[:, :, at] * p_ref[:, :, at] + q_ref[:, :, at]
            ref[:, j, base : base + 4, :] = west[:, 4 * f : 4 * f + 4, at]
            ref[:, j, base + 4 : base + 4 + CX, :] = own
            ref[:, j, base + 4 + CX : base + ROWS, :] = east[:, 4 * f : 4 * f + 4, at]
        for i in range(30):
            k, t = divmod(i, 3)
            slot = 8 * f + i % 8
            up = roll(north[i // 8], -4 * slot, 1)
            down = roll(south[i // 8], 124 - 4 * slot, 1)
            rows = jnp.where(lane < 4, up, jnp.where(lane >= 124, down, 0.0))
            if t < 2:
                ref[k, 2, base + 4 + 8 * t : base + 12 + 8 * t, :] = rows
            else:
                ref[k, 2, base + 4 + CX : base + ROWS, :] = rows[0:4]
                ref[k, 2, base : base + 4, :] = rows[4:8]
    for k in range(NZ):
        c = [cond[k, j, MID, :] for j in range(3)]
        after, _ = beside_lanes(c)
        w_y = [harmonic(c[j], after[j]) for j in range(3)]
        _, w_back = beside_lanes(w_y)
        for j in range(3):
            wx[k, j, MID, :] = harmonic(c[j], cond[k, j, 9 : 9 + ROWS, :])
            wy[k, j] = w_y[j]
            wy_back[k, j] = w_back[j]
            diag = inv[k, j] + wx[k, j, MID, :] + wx[k, j, 7 : 7 + ROWS, :] + w_y[j] + w_back[j]
            if k > 0:
                diag = diag + wz[k - 1, j]
            if k < NZ - 1:
                w_z = VERTICAL * harmonic(c[j], cond[k + 1, j, MID, :])
                wz[k, j] = w_z
                diag = diag + w_z
            inv[k, j] = OMEGA_RELAX / (diag + (diag == 0.0).astype(F32))
    old, new = h0, h1
    for _ in range(ITERS):
        for k in range(NZ):
            h = [old[k, j, MID, :] for j in range(3)]
            after, before = beside_lanes(h)
            for j in range(3):
                total = rhs[k, j]
                if k > 0:
                    total = total + wz[k - 1, j] * old[k - 1, j, MID, :]
                if k < NZ - 1:
                    total = total + wz[k, j] * old[k + 1, j, MID, :]
                along_x = wx[k, j, MID, :] * old[k, j, 9 : 9 + ROWS, :] + wx[k, j, 7 : 7 + ROWS, :] * old[k, j, 7 : 7 + ROWS, :]
                along_y = wy[k, j] * after[j] + wy_back[k, j] * before[j]
                new[k, j, MID, :] = (1.0 - OMEGA_RELAX) * h[j] + inv[k, j] * (along_x + along_y + total)
        old, new = new, old
    flat[NZ * CX : NORTH, :] = jnp.zeros((16, CY), F32)
    for k in range(NZ):
        h = [old[k, j, OWN, :] for j in range(3)]
        after, before = beside_lanes(h)
        at = slice(CX * k, CX * k + CX)
        for j in range(2):
            lanes = slice(128 * j, 128 * j + 128)

            def put(first, value):
                flat[first + CX * k : first + CX * k + CX, lanes] = value

            final[k, :, lanes] = h[j]
            put(EAST, -wx[k, j, OWN, :] * (old[k, j, 13 : 13 + CX, :] - h[j]))
            flat[NZ * CX + k : NZ * CX + k + 1, lanes] = -wx[k, j, 11:12, :] * (h[j][0:1] - old[k, j, 11:12, :])
            put(NORTH, -wy[k, j, INNER, :] * (after[j] - h[j]))
            put(SOUTH, -wy_back[k, j, INNER, :] * (h[j] - before[j]))
            if k < NZ - 1:
                put(LEVEL, -wz[k, j, INNER, :] * (old[k + 1, j, OWN, :] - h[j] + 1.0))
            suction = jnp.maximum(-h[j], 0.0)
            put(SATUR, RESIDUAL_SAT + (1.0 - RESIDUAL_SAT) * lax.rsqrt(1.0 + suction * suction))
    head_copy = pltpu.make_async_copy(final, head_ref, sems.at[0])
    head_copy.start()
    coarse, fine = split(flat[...], 2)
    tab_ref[:, 0:CY] = coarse
    tab_ref[:, CY : 2 * CY] = fine
    counts = small_ref[16:17, :]
    first = 0
    for d, cap in enumerate((CAPX, CAPX, CAPY, CAPY)):
        count = jnp.sum(jnp.where(lane == d, counts, 0), axis=1, keepdims=True)
        live_ref[first : first + cap, :] = (index_of((cap, 128), 0) < count).astype(F32)
        first += cap

    def store(slot, record):
        live = live_ref[pl.ds(slot, 1), :] > 0.0
        kept[slot] = jnp.where(live, 0.0, record)
        sent[slot] = jnp.where(live, record, 0.0)

    def group_step(i, carry):
        advance_group(tab_ref, cell_ref, rec_ref, found, i * GROUP_SENT, GROUP_SENT, store)
        return carry

    lax.fori_loop(0, SENT // GROUP_SENT, group_step, 0)
    copy = pltpu.make_async_copy(kept, next_ref.at[pl.ds(0, SENT)], sems.at[1])
    copy.start()
    links = jnp.concatenate([small_ref[j : j + 1, :] for j in range(8)], axis=1)
    surface = jnp.concatenate(split(final[NZ - 1], 3), axis=0)
    at_links = jnp.dot(surface, one_hot(links & (CY - 1), 1024), preferred_element_type=F32)
    at_links = at_links[0:CX] + at_links[CX : 2 * CX] + at_links[2 * CX : 3 * CX]
    picked = jnp.where(index_of((CX, 1024), 0) == (links >> 8), at_links, 0.0)
    value = jnp.sum(picked, axis=0, keepdims=True)
    flow = jnp.maximum(value, 0.0) + jnp.log1p(jnp.exp(-jnp.abs(value)))
    flows = [
        jnp.concatenate([flow[:, 256 * d : 256 * d + 128], flow[:, 256 * d + 128 : 256 * d + 256]] * 4, axis=0)
        for d in range(4)
    ]
    for ref, par, low, cap in (
        (xe_ref, par_x, 0, CAPX),
        (xo_ref, 1 - par_x, 0, CAPX),
        (ye_ref, par_y, 2, CAPY),
        (yo_ref, 1 - par_y, 2, CAPY),
    ):
        base = 2 * CAPX if low else 0
        ref[0:cap] = sent[pl.ds(base + par * cap, cap)]
        ref[cap] = jnp.where(par == 0, flows[low], flows[low + 1])
    copy.wait()
    head_copy.wait()


def rest_kernel(tab_ref, rec_ref, cell_ref, prev_ref, next_ref, found, kept, sems):
    def store(slot, record):
        kept[slot - SENT] = record

    def copy_of(i):
        first = i * GROUP_KEEP
        return pltpu.make_async_copy(
            kept.at[pl.ds(first, GROUP_KEEP)], next_ref.at[pl.ds(SENT + first, GROUP_KEEP)], sems.at[i]
        )

    def group_step(i, carry):
        advance_group(tab_ref, cell_ref, rec_ref, found, SENT + i * GROUP_KEEP, GROUP_KEEP, store)
        copy_of(i).start()
        return carry

    lax.fori_loop(0, KEEP // GROUP_KEEP, group_step, 0)
    for i in range(KEEP // GROUP_KEEP):
        copy_of(i).wait()


def arrive_kernel(small_ref, xe_ref, xo_ref, ye_ref, yo_ref, prev_ref, next_ref, inflow_ref, sems):
    par_x, par_y = parities()
    copies = []
    for n, (ref, par, base, cap) in enumerate(
        (
            (xe_ref, 1 - par_x, PB, CAPX),
            (xo_ref, par_x, PB, CAPX),
            (ye_ref, 1 - par_y, PB + 2 * CAPX, CAPY),
            (yo_ref, par_y, PB + 2 * CAPX, CAPY),
        )
    ):
        copies.append(
            pltpu.make_async_copy(ref.at[pl.ds(0, cap)], next_ref.at[pl.ds(base + par * cap, cap)], sems.at[n])
        )
    for copy in copies:
        copy.start()
    x_even, x_odd = xe_ref[CAPX], xo_ref[CAPX]
    y_even, y_odd = ye_ref[CAPY], yo_ref[CAPY]
    arrivals = [
        jnp.where(par_x == 0, x_odd, x_even),
        jnp.where(par_x == 0, x_even, x_odd),
        jnp.where(par_y == 0, y_odd, y_even),
        jnp.where(par_y == 0, y_even, y_odd),
    ]
    flow = jnp.concatenate([a[r : r + 1] for a in arrivals for r in range(2)], axis=1)
    links = jnp.concatenate([small_ref[j : j + 1, :] for j in range(8, 16)], axis=1)
    spread = jnp.where(index_of((CX, 1024), 0) == (links >> 8), flow, 0.0)
    parts = jnp.concatenate(split(spread, 3), axis=0)
    hot = one_hot(links & (CY - 1), 1024)
    total = lax.dot_general(parts, hot, (((1,), (1,)), ((), ())), preferred_element_type=F32)
    inflow_ref[...] = total[0:CX] + total[CX : 2 * CX] + total[2 * CX : 3 * CX]
    for copy in copies:
        copy.wait()


VMEM = pl.BlockSpec(memory_space=pltpu.VMEM)
ANY = pl.BlockSpec(memory_space=pl.ANY)
LIMIT = pltpu.CompilerParams(vmem_limit_bytes=32 << 20)


def swap(size, first):
    pairs = []
    for i in range(first, size - 1, 2):
        pairs += [(i, i + 1), (i + 1, i)]
    return pairs


def exchange(even, odd, axis):
    size = lax.axis_size(axis)
    from_odd = lax.ppermute(odd, axis, swap(size, 1))
    from_even = lax.ppermute(even, axis, swap(size, 0))
    return from_even, from_odd


def shape(*dims, dtype=F32):
    return jax.ShapeDtypeStruct(dims, dtype)


def body(
    pressure, conductivity, storage, source, particles, crossing, particle_cell, river_source, river_target
):
    counts = jnp.pad(crossing.reshape(1, 4), ((0, 7), (0, 124)))
    small = jnp.concatenate([river_source.reshape(8, 128), river_target.reshape(8, 128), counts], axis=0)
    grid = (pressure, conductivity, storage, source)
    tile = pltpu.VMEM((NZ, CX, CY), F32)
    x_even, x_odd = pl.pallas_call(
        edge_rows_kernel,
        out_shape=(shape(NZ, CX, CY), shape(NZ, CX, CY)),
        in_specs=[ANY] * 4,
        out_specs=(ANY, ANY),
        scratch_shapes=[tile] * 6 + [pltpu.SemaphoreType.DMA((2, 6))],
        compiler_params=pltpu.CompilerParams(vmem_limit_bytes=60 << 20),
        name="edge_rows",
    )(*grid)
    halo_x = exchange(x_even, x_odd, "gx")
    y_even, y_odd = pl.pallas_call(
        edge_lanes_kernel,
        out_shape=(shape(4, 8, 128), shape(4, 8, 128)),
        in_specs=[VMEM] * 6,
        out_specs=(VMEM, VMEM),
        compiler_params=LIMIT,
        name="edge_lanes",
    )(*grid, *halo_x)
    halo_y = exchange(y_even, y_odd, "gy")
    records = particles[0, 0]
    cells = particle_cell[0, 0]
    tall = pltpu.VMEM((NZ, 3, TALL, 128), F32)
    field = pltpu.VMEM((NZ, 3, ROWS, 128), F32)
    head, table, moved, x_even, x_odd, y_even, y_odd = pl.pallas_call(
        sweep_kernel,
        out_shape=(
            shape(NZ, CX, CY),
            shape(TABLE, 2 * CY, dtype=BF16),
            shape(OUT, 8, 128),
            shape(CAPX + 1, 8, 128),
            shape(CAPX + 1, 8, 128),
            shape(CAPY + 1, 8, 128),
            shape(CAPY + 1, 8, 128),
        ),
        in_specs=[VMEM] * 11,
        out_specs=(ANY, VMEM, ANY) + (VMEM,) * 4,
        scratch_shapes=[tall] * 4
        + [field] * 5
        + [
            pltpu.VMEM((TABLE, CY), F32),
            pltpu.VMEM((TABLE, 128 * GROUP_SENT), F32),
            pltpu.VMEM((SENT, 8, 128), F32),
            pltpu.VMEM((SENT, 8, 128), F32),
            tile,
            pltpu.VMEM((SENT, 128), F32),
            pltpu.SemaphoreType.DMA((2,)),
        ],
        compiler_params=LIMIT,
        name="sweep",
    )(small, *grid, *halo_x, *halo_y, records, cells)
    x_even, x_odd = exchange(x_even, x_odd, "gx")
    y_even, y_odd = exchange(y_even, y_odd, "gy")
    moved = pl.pallas_call(
        rest_kernel,
        out_shape=shape(OUT, 8, 128),
        in_specs=[VMEM] * 3 + [ANY],
        out_specs=ANY,
        scratch_shapes=[pltpu.VMEM((TABLE, 128 * GROUP_KEEP), F32), pltpu.VMEM((KEEP, 8, 128), F32), pltpu.SemaphoreType.DMA((KEEP // GROUP_KEEP,))],
        input_output_aliases={3: 0},
        compiler_params=LIMIT,
        cost_estimate=pl.CostEstimate(
            flops=2 * TABLE * 512 * 128 * KEEP, bytes_accessed=4 << 20, transcendentals=0
        ),
        name="rest",
    )(table, records, cells, moved)
    moved, inflow = pl.pallas_call(
        arrive_kernel,
        out_shape=(shape(OUT, 8, 128), shape(CX, CY)),
        in_specs=[VMEM] * 5 + [ANY],
        out_specs=(ANY, VMEM),
        scratch_shapes=[pltpu.SemaphoreType.DMA((4,))],
        input_output_aliases={5: 0},
        compiler_params=LIMIT,
        name="arrive",
    )(small, x_even, x_odd, y_even, y_odd, moved)
    return head, moved[None, None], inflow


def solution(mesh):
    in_specs = (
        P(None, "gx", "gy"),
        P(None, "gx", "gy"),
        P(None, "gx", "gy"),
        P(None, "gx", "gy"),
        P("gx", "gy", None, None, None),
        P("gx", "gy", None),
        P("gx", "gy", None, None),
        P("gx", "gy", None, None, None),
        P("gx", "gy", None, None, None),
    )
    out_specs = (P(None, "gx", "gy"), P("gx", "gy", None, None, None), P("gx", "gy"))
    return jax.shard_map(body, mesh=mesh, in_specs=in_specs, out_specs=out_specs, check_vma=False)
```

```python
import functools

import jax
import jax.numpy as jnp
from jax import lax
from jax.experimental import pallas as pl
from jax.experimental.pallas import tpu as pltpu
from jax.sharding import PartitionSpec as P

F32 = jnp.float32
BF16 = jnp.bfloat16

ITERS = 4
CAPX = 16
CAPY = 4
NZ = 10
CX = 16
CY = 256
PB = 104
SENT = 2 * CAPX + 2 * CAPY
KEEP = PB - SENT
OUT = PB + SENT
GROUP_SENT = 20
GROUP_KEEP = 16

OMEGA_RELAX = 0.8
VERTICAL = 4.0
POROSITY = 0.4
RESIDUAL_SAT = 0.1
TIME_STEP = 0.01
DECAY_RATE = 20.0

ROWS = CX + 8
TALL = 8 + ROWS + 8
MID = slice(8, 8 + ROWS)
OWN = slice(12, 12 + CX)
INNER = slice(4, 4 + CX)

EAST = 0
NORTH = 176
SOUTH = 336
LEVEL = 496
SATUR = 640
TABLE = 800


def harmonic(left, right):
    total = left + right
    return 2.0 * left * right / (total + (total == 0.0).astype(total.dtype))


def index_of(shape, axis):
    return lax.broadcasted_iota(jnp.int32, shape, axis)


def roll(x, shift, axis):
    return pltpu.roll(x, shift % x.shape[axis], axis)


def in_grid(axis):
    here = lax.axis_index(axis)
    return jnp.where((here == 0) | (here == lax.axis_size(axis) - 1), 0, 1)


def parities():
    return lax.rem(lax.axis_index("gx"), 2), lax.rem(lax.axis_index("gy"), 2)


def edge_rows_kernel(p_hbm, c_hbm, s_hbm, q_hbm, even_hbm, odd_hbm, p_ref, c_ref, s_ref, q_ref, even_ref, odd_ref, sems):
    halves = (slice(0, NZ // 2), slice(NZ // 2, NZ))
    loads = []
    for h, part in enumerate(halves):
        pairs = ((p_hbm, p_ref), (c_hbm, c_ref), (s_hbm, s_ref), (q_hbm, q_ref))
        loads.append([pltpu.make_async_copy(a.at[part], b.at[part], sems.at[h, n]) for n, (a, b) in enumerate(pairs)])
        for copy in loads[h]:
            copy.start()
    parity = parities()[0]
    within = in_grid("gx")
    row = index_of((1, 8, CY), 1)
    stores = []
    for h, part in enumerate(halves):
        for copy in loads[h]:
            copy.wait()
        pieces = []
        for start, step, outer in ((0, -1, 3), (8, 1, 4)):
            tile = slice(start, start + 8)
            p, c, s, q = (ref[part, tile, :] for ref in (p_ref, c_ref, s_ref, q_ref))
            weight = jnp.where(row == outer, harmonic(c, roll(c, step, 1)), 0.0)
            rhs = s * p + q + weight * roll(p, step, 1)
            side = slice(0, 4) if start == 0 else slice(4, 8)
            pieces.append(jnp.concatenate([p[:, side], c[:, side], (s + weight)[:, side], rhs[:, side]], axis=1))
        west, east = pieces
        even_ref[part] = jnp.where(parity == 0, east, west)
        odd_ref[part] = jnp.where(within == 0, 0.0, jnp.where(parity == 0, west, east))
        for n, (a, b) in enumerate(((even_ref, even_hbm), (odd_ref, odd_hbm))):
            copy = pltpu.make_async_copy(a.at[part], b.at[part], sems.at[h, 4 + n])
            copy.start()
            stores.append(copy)
    for copy in stores:
        copy.wait()


def beside_rows(from_even, from_odd, par_x):
    east = jnp.where(par_x == 0, from_even, from_odd)
    west = jnp.where(par_x == 0, from_odd, from_even)
    return [jnp.concatenate([east[:, 4 * f : 4 * f + 4], west[:, 4 * f : 4 * f + 4]], axis=1) for f in range(4)]


def edge_lanes_kernel(p_ref, c_ref, s_ref, q_ref, re_ref, ro_ref, even_ref, odd_ref):
    par_x, par_y = parities()
    lane = index_of((1, 1, 128), 2)
    packed = []
    for start, step, outer, low in ((0, -1, 3, 0), (128, 1, 124, 124)):
        at = slice(start, start + 128)
        near = beside_rows(re_ref[:, :, at], ro_ref[:, :, at], par_x)
        p, c, s, q = (ref[:, :, at] for ref in (p_ref, c_ref, s_ref, q_ref))
        p, c, s, r = (jnp.concatenate(pair, axis=1) for pair in zip((p, c, s, s * p + q), near))
        weight = jnp.where(lane == outer, harmonic(c, roll(c, step, 2)), 0.0)
        fields = [p, c, s + weight, r + weight * roll(p, step, 2)]
        inside = (lane >= low) & (lane < low + 4)
        total = [jnp.zeros((8, 128), F32) for _ in range(4)]
        for f in range(4):
            rows = jnp.where(inside, fields[f], 0.0).reshape(30, 8, 128)
            for i in range(30):
                slot = 8 * f + i % 8
                total[i // 8] = total[i // 8] + roll(rows[i], 4 * slot - low, 1)
        packed.append(total)
    south, north = packed
    within = in_grid("gy")
    for j in range(4):
        even_ref[j] = jnp.where(par_y == 0, north[j], south[j])
        odd_ref[j] = jnp.where(within == 0, 0.0, jnp.where(par_y == 0, south[j], north[j]))


def one_hot(values, lanes):
    hit = index_of((CY, lanes), 0).astype(BF16) == values.astype(BF16)
    return jnp.where(hit, jnp.ones((), BF16), jnp.zeros((), BF16))


def split(x, parts):
    out = []
    for _ in range(parts):
        piece = x.astype(BF16)
        out.append(piece)
        x = x - piece.astype(F32)
    return out


def sample(tab_ref, cells, found_ref):
    lanes = cells.shape[1]
    hot = one_hot(cells & (CY - 1), lanes)
    found_ref[...] = jnp.dot(tab_ref[...], jnp.concatenate([hot, hot], 0), preferred_element_type=F32)
    high = cells >> 8
    column = high & (CX - 1)
    west_row = jnp.where(column == 0, NZ * CX + (high >> 4), high - 1)
    here = jnp.broadcast_to(high >> 3, (8, lanes))
    beside = jnp.broadcast_to(west_row >> 3, (8, lanes))
    west = east = north = south = top = bottom = satur = jnp.zeros((8, lanes), F32)
    for g in range(22):
        at = 8 * g
        face = found_ref[at : at + 8, :]
        west = jnp.where(beside == g, face, west)
        if g < 20:
            mask = here == g
            east = jnp.where(mask, face, east)
            north = jnp.where(mask, found_ref[NORTH + at : NORTH + at + 8, :], north)
            south = jnp.where(mask, found_ref[SOUTH + at : SOUTH + at + 8, :], south)
            satur = jnp.where(mask, found_ref[SATUR + at : SATUR + at + 8, :], satur)
            if g < 18:
                top = jnp.where(mask, found_ref[LEVEL + at : LEVEL + at + 8, :], top)
            if g >= 2:
                bottom = jnp.where(mask, found_ref[LEVEL + at - 16 : LEVEL + at - 8, :], bottom)
    row = index_of((8, lanes), 0)
    own = row == (high & 7)
    other = row == (west_row & 7)

    def pick(mask, rows):
        return jnp.sum(jnp.where(mask, rows, 0.0), axis=0, keepdims=True)

    return [pick(other, west)] + [pick(own, v) for v in (east, south, north, bottom, top, satur)]


def advance(record, sampled):
    west, east, south, north, bottom, top, satur = sampled
    scale = TIME_STEP / (POROSITY * satur)
    move_x = scale * (west + record[0:1] * (east - west))
    move_y = scale * (south + record[1:2] * (north - south))
    move_z = scale * (bottom + record[2:3] * (top - bottom))
    row = index_of(record.shape, 0)
    step = jnp.where(
        (row == 0) | (row == 6),
        move_x,
        jnp.where((row == 1) | (row == 7), move_y, jnp.where(row == 2, move_z, TIME_STEP)),
    )
    decayed = record * jnp.exp(-DECAY_RATE * TIME_STEP * satur)
    return jnp.where(row == 4, decayed, jnp.where(row == 5, satur, record + step))


def advance_group(tab_ref, cell_ref, rec_ref, found_ref, first, size, store):
    cells = jnp.concatenate([cell_ref[pl.ds(first + j, 1), :] for j in range(size)], axis=1)
    sampled = sample(tab_ref, cells, found_ref)
    for j in range(size):
        mine = [v[:, 128 * j : 128 * j + 128] for v in sampled]
        store(first + j, advance(rec_ref[first + j], mine))


def beside_lanes(tiles):
    lane = index_of(tiles[0].shape, 1)
    ahead = [roll(t, -1, 1) for t in tiles]
    back = [roll(t, 1, 1) for t in tiles]
    after = [jnp.where(lane == 127, ahead[(j + 1) % 3], ahead[j]) for j in range(3)]
    before = [jnp.where(lane == 0, back[(j + 2) % 3], back[j]) for j in range(3)]
    return after, before


def sweep_kernel(
    small_ref, p_ref, c_ref, s_ref, q_ref, rxe_ref, rxo_ref, rye_ref, ryo_ref, rec_ref, cell_ref,
    head_ref, tab_ref, kept, xe_ref, xo_ref, ye_ref, yo_ref,
    h0, h1, cond, wx, rhs, inv, wy, wy_back, wz, flat, found, sent, final, live_ref, sem,
):
    par_x, par_y = parities()
    edge = jnp.zeros((NZ, 3, 8, 128), F32)
    for ref in (h0, h1, cond, wx):
        ref[:, :, 0:8, :] = edge
        ref[:, :, 8 + ROWS : TALL, :] = edge
    east = jnp.where(par_x == 0, rxe_ref[...], rxo_ref[...])
    west = jnp.where(par_x == 0, rxo_ref[...], rxe_ref[...])
    north = [jnp.where(par_y == 0, rye_ref[j], ryo_ref[j]) for j in range(4)]
    south = [jnp.where(par_y == 0, ryo_ref[j], rye_ref[j]) for j in range(4)]
    lane = index_of((1, 128), 1)
    for f, (ref, base) in enumerate(((h0, 8), (cond, 8), (inv, 0), (rhs, 0))):
        for j in range(2):
            at = slice(128 * j, 128 * j + 128)
            own = (p_ref, c_ref, s_ref)[f][:, :, at] if f < 3 else s_ref[:, :, at] * p_ref[:, :, at] + q_ref[:, :, at]
            ref[:, j, base : base + 4, :] = west[:, 4 * f : 4 * f + 4, at]
            ref[:, j, base + 4 : base + 4 + CX, :] = own
            ref[:, j, base + 4 + CX : base + ROWS, :] = east[:, 4 * f : 4 * f + 4, at]
        for i in range(30):
            k, t = divmod(i, 3)
            slot = 8 * f + i % 8
            up = roll(north[i // 8], -4 * slot, 1)
            down = roll(south[i // 8], 124 - 4 * slot, 1)
            rows = jnp.where(lane < 4, up, jnp.where(lane >= 124, down, 0.0))
            if t < 2:
                ref[k, 2, base + 4 + 8 * t : base + 12 + 8 * t, :] = rows
            else:
                ref[k, 2, base + 4 + CX : base + ROWS, :] = rows[0:4]
                ref[k, 2, base : base + 4, :] = rows[4:8]
    for k in range(NZ):
        c = [cond[k, j, MID, :] for j in range(3)]
        after, _ = beside_lanes(c)
        w_y = [harmonic(c[j], after[j]) for j in range(3)]
        _, w_back = beside_lanes(w_y)
        for j in range(3):
            wx[k, j, MID, :] = harmonic(c[j], cond[k, j, 9 : 9 + ROWS, :])
            wy[k, j] = w_y[j]
            wy_back[k, j] = w_back[j]
            diag = inv[k, j] + wx[k, j, MID, :] + wx[k, j, 7 : 7 + ROWS, :] + w_y[j] + w_back[j]
            if k > 0:
                diag = diag + wz[k - 1, j]
            if k < NZ - 1:
                w_z = VERTICAL * harmonic(c[j], cond[k + 1, j, MID, :])
                wz[k, j] = w_z
                diag = diag + w_z
            inv[k, j] = OMEGA_RELAX / (diag + (diag == 0.0).astype(F32))
    old, new = h0, h1
    for _ in range(ITERS):
        for k in range(NZ):
            h = [old[k, j, MID, :] for j in range(3)]
            after, before = beside_lanes(h)
            for j in range(3):
                total = rhs[k, j]
                if k > 0:
                    total = total + wz[k - 1, j] * old[k - 1, j, MID, :]
                if k < NZ - 1:
                    total = total + wz[k, j] * old[k + 1, j, MID, :]
                along_x = wx[k, j, MID, :] * old[k, j, 9 : 9 + ROWS, :] + wx[k, j, 7 : 7 + ROWS, :] * old[k, j, 7 : 7 + ROWS, :]
                along_y = wy[k, j] * after[j] + wy_back[k, j] * before[j]
                new[k, j, MID, :] = (1.0 - OMEGA_RELAX) * h[j] + inv[k, j] * (along_x + along_y + total)
        old, new = new, old
    flat[NZ * CX : NORTH, :] = jnp.zeros((16, CY), F32)
    for k in range(NZ):
        h = [old[k, j, OWN, :] for j in range(3)]
        after, before = beside_lanes(h)
        at = slice(CX * k, CX * k + CX)
        for j in range(2):
            lanes = slice(128 * j, 128 * j + 128)

            def put(first, value):
                flat[first + CX * k : first + CX * k + CX, lanes] = value

            final[k, :, lanes] = h[j]
            put(EAST, -wx[k, j, OWN, :] * (old[k, j, 13 : 13 + CX, :] - h[j]))
            flat[NZ * CX + k : NZ * CX + k + 1, lanes] = -wx[k, j, 11:12, :] * (h[j][0:1] - old[k, j, 11:12, :])
            put(NORTH, -wy[k, j, INNER, :] * (after[j] - h[j]))
            put(SOUTH, -wy_back[k, j, INNER, :] * (h[j] - before[j]))
            if k < NZ - 1:
                put(LEVEL, -wz[k, j, INNER, :] * (old[k + 1, j, OWN, :] - h[j] + 1.0))
            suction = jnp.maximum(-h[j], 0.0)
            put(SATUR, RESIDUAL_SAT + (1.0 - RESIDUAL_SAT) * lax.rsqrt(1.0 + suction * suction))
    head_copy = pltpu.make_async_copy(final, head_ref, sem)
    head_copy.start()
    coarse, fine = split(flat[...], 2)
    tab_ref[:, 0:CY] = coarse
    tab_ref[:, CY : 2 * CY] = fine
    counts = small_ref[16:17, :]
    first = 0
    for d, cap in enumerate((CAPX, CAPX, CAPY, CAPY)):
        count = jnp.sum(jnp.where(lane == d, counts, 0), axis=1, keepdims=True)
        live_ref[first : first + cap, :] = (index_of((cap, 128), 0) < count).astype(F32)
        first += cap

    def store(slot, record):
        live = live_ref[pl.ds(slot, 1), :] > 0.0
        kept[slot] = jnp.where(live, 0.0, record)
        sent[slot] = jnp.where(live, record, 0.0)

    def group_step(i, carry):
        advance_group(tab_ref, cell_ref, rec_ref, found, i * GROUP_SENT, GROUP_SENT, store)
        return carry

    lax.fori_loop(0, SENT // GROUP_SENT, group_step, 0)
    links = jnp.concatenate([small_ref[j : j + 1, :] for j in range(8)], axis=1)
    surface = jnp.concatenate(split(final[NZ - 1], 3), axis=0)
    at_links = jnp.dot(surface, one_hot(links & (CY - 1), 1024), preferred_element_type=F32)
    at_links = at_links[0:CX] + at_links[CX : 2 * CX] + at_links[2 * CX : 3 * CX]
    picked = jnp.where(index_of((CX, 1024), 0) == (links >> 8), at_links, 0.0)
    value = jnp.sum(picked, axis=0, keepdims=True)
    flow = jnp.maximum(value, 0.0) + jnp.log1p(jnp.exp(-jnp.abs(value)))
    flows = [
        jnp.concatenate([flow[:, 256 * d : 256 * d + 128], flow[:, 256 * d + 128 : 256 * d + 256]] * 4, axis=0)
        for d in range(4)
    ]
    for ref, par, low, cap, within in (
        (xe_ref, par_x, 0, CAPX, None),
        (xo_ref, 1 - par_x, 0, CAPX, in_grid("gx")),
        (ye_ref, par_y, 2, CAPY, None),
        (yo_ref, 1 - par_y, 2, CAPY, in_grid("gy")),
    ):
        base = 2 * CAPX if low else 0
        leaving = sent[pl.ds(base + par * cap, cap)]
        flow_out = jnp.where(par == 0, flows[low], flows[low + 1])
        ref[0:cap] = leaving if within is None else jnp.where(within == 0, 0.0, leaving)
        ref[cap] = flow_out if within is None else jnp.where(within == 0, 0.0, flow_out)
    head_copy.wait()


def rest_kernel(first, tab_ref, rec_ref, cell_ref, *refs):
    kept, found = refs[-2:]

    def store(slot, record):
        kept[slot - first] = record

    advance_group(tab_ref, cell_ref, rec_ref, found, first, GROUP_KEEP, store)


def arrive_kernel(small_ref, xe_ref, xo_ref, ye_ref, yo_ref, *refs):
    kept = refs[:-3]
    next_ref, inflow_ref, sems = refs[-3:]
    par_x, par_y = parities()
    copies = []

    def send(source, first, count):
        copy = pltpu.make_async_copy(source, next_ref.at[pl.ds(first, count)], sems.at[len(copies)])
        copy.start()
        copies.append(copy)

    send(kept[0], 0, SENT)
    for n, ref in enumerate(kept[1:]):
        send(ref, SENT + n * GROUP_KEEP, GROUP_KEEP)
    for ref, par, base, cap in (
        (xe_ref, 1 - par_x, PB, CAPX),
        (xo_ref, par_x, PB, CAPX),
        (ye_ref, 1 - par_y, PB + 2 * CAPX, CAPY),
        (yo_ref, par_y, PB + 2 * CAPX, CAPY),
    ):
        send(ref.at[pl.ds(0, cap)], base + par * cap, cap)
    x_even, x_odd = xe_ref[CAPX], xo_ref[CAPX]
    y_even, y_odd = ye_ref[CAPY], yo_ref[CAPY]
    arrivals = [
        jnp.where(par_x == 0, x_odd, x_even),
        jnp.where(par_x == 0, x_even, x_odd),
        jnp.where(par_y == 0, y_odd, y_even),
        jnp.where(par_y == 0, y_even, y_odd),
    ]
    flow = jnp.concatenate([a[r : r + 1] for a in arrivals for r in range(2)], axis=1)
    links = jnp.concatenate([small_ref[j : j + 1, :] for j in range(8, 16)], axis=1)
    spread = jnp.where(index_of((CX, 1024), 0) == (links >> 8), flow, 0.0)
    parts = jnp.concatenate(split(spread, 3), axis=0)
    hot = one_hot(links & (CY - 1), 1024)
    total = lax.dot_general(parts, hot, (((1,), (1,)), ((), ())), preferred_element_type=F32)
    inflow_ref[...] = total[0:CX] + total[CX : 2 * CX] + total[2 * CX : 3 * CX]
    for copy in copies:
        copy.wait()


VMEM = pl.BlockSpec(memory_space=pltpu.VMEM)
ANY = pl.BlockSpec(memory_space=pl.ANY)
LIMIT = pltpu.CompilerParams(vmem_limit_bytes=32 << 20)


AXES = ("gx", "gy")


def swap(value, axis, first):
    sizes = [lax.axis_size(name) for name in AXES]
    along, across = AXES.index(axis), 1 - AXES.index(axis)

    def place(i, other):
        at = (i, other) if along == 0 else (other, i)
        return at[0] * sizes[1] + at[1]

    pairs = []
    for other in range(sizes[across]):
        for i in range(first, sizes[along] - 1, 2):
            pairs.append((place(i, other), place(i + 1, other)))
    if first:
        for end in (0, sizes[along] - 1):
            for other in range(0, sizes[across], 2):
                pairs.append((place(end, other), place(end, other + 1)))
    return lax.ppermute(value, AXES, pairs + [(b, a) for a, b in pairs])


def exchange(even, odd, axis):
    from_odd = swap(odd, axis, 1)
    from_even = swap(even, axis, 0)
    return from_even, from_odd


def shape(*dims, dtype=F32):
    return jax.ShapeDtypeStruct(dims, dtype)


def body(
    pressure, conductivity, storage, source, particles, crossing, particle_cell, river_source, river_target
):
    counts = jnp.pad(crossing.reshape(1, 4), ((0, 7), (0, 124)))
    small = jnp.concatenate([river_source.reshape(8, 128), river_target.reshape(8, 128), counts], axis=0)
    grid = (pressure, conductivity, storage, source)
    tile = pltpu.VMEM((NZ, CX, CY), F32)
    x_even, x_odd = pl.pallas_call(
        edge_rows_kernel,
        out_shape=(shape(NZ, CX, CY), shape(NZ, CX, CY)),
        in_specs=[ANY] * 4,
        out_specs=(ANY, ANY),
        scratch_shapes=[tile] * 6 + [pltpu.SemaphoreType.DMA((2, 6))],
        compiler_params=pltpu.CompilerParams(vmem_limit_bytes=60 << 20),
        name="edge_rows",
    )(*grid)
    halo_x = exchange(x_even, x_odd, "gx")
    y_even, y_odd = pl.pallas_call(
        edge_lanes_kernel,
        out_shape=(shape(4, 8, 128), shape(4, 8, 128)),
        in_specs=[VMEM] * 6,
        out_specs=(VMEM, VMEM),
        compiler_params=LIMIT,
        name="edge_lanes",
    )(*grid, *halo_x)
    halo_y = exchange(y_even, y_odd, "gy")
    records = particles[0, 0]
    cells = particle_cell[0, 0]
    tall = pltpu.VMEM((NZ, 3, TALL, 128), F32)
    field = pltpu.VMEM((NZ, 3, ROWS, 128), F32)
    head, table, kept, x_even, x_odd, y_even, y_odd = pl.pallas_call(
        sweep_kernel,
        out_shape=(
            shape(NZ, CX, CY),
            shape(TABLE, 2 * CY, dtype=BF16),
            shape(SENT, 8, 128),
            shape(CAPX + 1, 8, 128),
            shape(CAPX + 1, 8, 128),
            shape(CAPY + 1, 8, 128),
            shape(CAPY + 1, 8, 128),
        ),
        in_specs=[VMEM] * 11,
        out_specs=(ANY,) + (VMEM,) * 6,
        scratch_shapes=[tall] * 4
        + [field] * 5
        + [
            pltpu.VMEM((TABLE, CY), F32),
            pltpu.VMEM((TABLE, 128 * GROUP_SENT), F32),
            pltpu.VMEM((SENT, 8, 128), F32),
            tile,
            pltpu.VMEM((SENT, 128), F32),
            pltpu.SemaphoreType.DMA,
        ],
        compiler_params=LIMIT,
        name="sweep",
    )(small, *grid, *halo_x, *halo_y, records, cells)
    payloads = [
        (x_odd, "gx", 1),
        (y_even, "gy", 0),
        (y_odd, "gy", 1),
        (x_even, "gx", 0),
    ]
    received = []
    done = [kept]
    waiting = payloads[0][0]
    for n, (_, axis, first) in enumerate(payloads):
        received.append(swap(waiting, axis, first))
        later = [payloads[n + 1][0]] if n + 1 < len(payloads) else []
        outs = pl.pallas_call(
            functools.partial(rest_kernel, SENT + n * GROUP_KEEP),
            out_shape=[jax.ShapeDtypeStruct(v.shape, v.dtype) for v in later] + [shape(GROUP_KEEP, 8, 128)],
            in_specs=[VMEM] * (3 + len(later)),
            out_specs=[VMEM] * (1 + len(later)),
            scratch_shapes=[pltpu.VMEM((TABLE, 128 * GROUP_KEEP), F32)],
            input_output_aliases={3: 0} if later else {},
            compiler_params=LIMIT,
            cost_estimate=pl.CostEstimate(
                flops=2 * TABLE * 512 * 128 * GROUP_KEEP, bytes_accessed=1 << 20, transcendentals=0
            ),
            name=f"rest_{n}",
        )(table, records, cells, *later)
        done.append(outs[-1])
        waiting = outs[0]
    from_x_odd, from_y_even, from_y_odd, from_x_even = received
    moved, inflow = pl.pallas_call(
        arrive_kernel,
        out_shape=(shape(OUT, 8, 128), shape(CX, CY)),
        in_specs=[VMEM] * (5 + len(done)),
        out_specs=(ANY, VMEM),
        scratch_shapes=[pltpu.SemaphoreType.DMA((4 + len(done),))],
        compiler_params=LIMIT,
        name="arrive",
    )(small, from_x_even, from_x_odd, from_y_even, from_y_odd, *done)
    return head, moved[None, None], inflow


def solution(mesh):
    in_specs = (
        P(None, "gx", "gy"),
        P(None, "gx", "gy"),
        P(None, "gx", "gy"),
        P(None, "gx", "gy"),
        P("gx", "gy", None, None, None),
        P("gx", "gy", None),
        P("gx", "gy", None, None),
        P("gx", "gy", None, None, None),
        P("gx", "gy", None, None, None),
    )
    out_specs = (P(None, "gx", "gy"), P("gx", "gy", None, None, None), P("gx", "gy"))
    return jax.shard_map(body, mesh=mesh, in_specs=in_specs, out_specs=out_specs, check_vma=False)
```

```python
import functools

import jax
import jax.numpy as jnp
from jax import lax
from jax.experimental import pallas as pl
from jax.experimental.pallas import tpu as pltpu
from jax.sharding import PartitionSpec as P

F32 = jnp.float32
BF16 = jnp.bfloat16

ITERS = 4
CAPX = 16
CAPY = 4
NZ = 10
CX = 16
CY = 256
PB = 104
SENT = 2 * CAPX + 2 * CAPY
KEEP = PB - SENT
OUT = PB + SENT
GROUP_SENT = 20
GROUPS_KEEP = (16, 16, 32)

OMEGA_RELAX = 0.8
VERTICAL = 4.0
POROSITY = 0.4
RESIDUAL_SAT = 0.1
TIME_STEP = 0.01
DECAY_RATE = 20.0

ROWS = CX + 8
TALL = 8 + ROWS + 8
MID = slice(8, 8 + ROWS)
OWN = slice(12, 12 + CX)
INNER = slice(4, 4 + CX)

EAST = 0
NORTH = 176
SOUTH = 336
LEVEL = 496
SATUR = 640
TABLE = 800


def harmonic(left, right):
    total = left + right
    return 2.0 * left * right / (total + (total == 0.0).astype(total.dtype))


def index_of(shape, axis):
    return lax.broadcasted_iota(jnp.int32, shape, axis)


def roll(x, shift, axis):
    return pltpu.roll(x, shift % x.shape[axis], axis)


def in_grid(axis):
    here = lax.axis_index(axis)
    return jnp.where((here == 0) | (here == lax.axis_size(axis) - 1), 0, 1)


def parities():
    return lax.rem(lax.axis_index("gx"), 2), lax.rem(lax.axis_index("gy"), 2)


def edge_of(p, c, s, q, low):
    step, outer = (-1, 3) if low else (1, 4)
    weight = jnp.where(index_of((1, 8, CY), 1) == outer, harmonic(c, roll(c, step, 1)), 0.0)
    rhs = s * p + q + weight * roll(p, step, 1)
    side = slice(0, 4) if low else slice(4, 8)
    return jnp.concatenate([p[:, side], c[:, side], (s + weight)[:, side], rhs[:, side]], axis=1)


def odd_rows_kernel(p_hbm, c_hbm, s_hbm, q_hbm, odd_ref, p_ref, c_ref, s_ref, q_ref, sems):
    parity = parities()[0]
    within = in_grid("gx")
    pairs = ((p_hbm, p_ref), (c_hbm, c_ref), (s_hbm, s_ref), (q_hbm, q_ref))
    loads = []
    for h, tile in enumerate((parity, 1 - parity)):
        rows = pl.ds(pl.multiple_of(8 * tile, 8), 8)
        for n, (source, ref) in enumerate(pairs):
            copy = pltpu.make_async_copy(source.at[:, rows, :], ref.at[:, rows, :], sems.at[h, n])
            copy.start()
            loads.append(copy)
    for copy in loads[:4]:
        copy.wait()
    rows = pl.ds(pl.multiple_of(8 * parity, 8), 8)
    fields = [ref[:, rows, :] for _, ref in pairs]
    edge = jnp.where(parity == 0, edge_of(*fields, True), edge_of(*fields, False))
    odd_ref[...] = jnp.where(within == 0, 0.0, edge)
    for copy in loads[4:]:
        copy.wait()


def even_rows_kernel(p_ref, c_ref, s_ref, q_ref, even_ref):
    parity = parities()[0]
    refs = (p_ref, c_ref, s_ref, q_ref)
    west = edge_of(*(ref[:, 0:8, :] for ref in refs), True)
    east = edge_of(*(ref[:, 8:16, :] for ref in refs), False)
    even_ref[...] = jnp.where(parity == 0, east, west)


def beside_rows(from_even, from_odd, par_x):
    east = jnp.where(par_x == 0, from_even, from_odd)
    west = jnp.where(par_x == 0, from_odd, from_even)
    return [jnp.concatenate([east[:, 4 * f : 4 * f + 4], west[:, 4 * f : 4 * f + 4]], axis=1) for f in range(4)]


def edge_lanes_kernel(p_ref, c_ref, s_ref, q_ref, re_ref, ro_ref, even_ref, odd_ref):
    par_x, par_y = parities()
    lane = index_of((1, 1, 128), 2)
    packed = []
    for start, step, outer, low in ((0, -1, 3, 0), (128, 1, 124, 124)):
        at = slice(start, start + 128)
        near = beside_rows(re_ref[:, :, at], ro_ref[:, :, at], par_x)
        p, c, s, q = (ref[:, :, at] for ref in (p_ref, c_ref, s_ref, q_ref))
        p, c, s, r = (jnp.concatenate(pair, axis=1) for pair in zip((p, c, s, s * p + q), near))
        weight = jnp.where(lane == outer, harmonic(c, roll(c, step, 2)), 0.0)
        fields = [p, c, s + weight, r + weight * roll(p, step, 2)]
        inside = (lane >= low) & (lane < low + 4)
        total = [jnp.zeros((8, 128), F32) for _ in range(4)]
        for f in range(4):
            rows = jnp.where(inside, fields[f], 0.0).reshape(30, 8, 128)
            for i in range(30):
                slot = 8 * f + i % 8
                total[i // 8] = total[i // 8] + roll(rows[i], 4 * slot - low, 1)
        packed.append(total)
    south, north = packed
    within = in_grid("gy")
    for j in range(4):
        even_ref[j] = jnp.where(par_y == 0, north[j], south[j])
        odd_ref[j] = jnp.where(within == 0, 0.0, jnp.where(par_y == 0, south[j], north[j]))


def one_hot(values, lanes):
    hit = index_of((CY, lanes), 0).astype(BF16) == values.astype(BF16)
    return jnp.where(hit, jnp.ones((), BF16), jnp.zeros((), BF16))


def split(x, parts):
    out = []
    for _ in range(parts):
        piece = x.astype(BF16)
        out.append(piece)
        x = x - piece.astype(F32)
    return out


def sample(tab_ref, cells, found_ref):
    lanes = cells.shape[1]
    hot = one_hot(cells & (CY - 1), lanes)
    found_ref[...] = jnp.dot(tab_ref[...], jnp.concatenate([hot, hot], 0), preferred_element_type=F32)
    high = cells >> 8
    column = high & (CX - 1)
    west_row = jnp.where(column == 0, NZ * CX + (high >> 4), high - 1)
    here = jnp.broadcast_to(high >> 3, (8, lanes))
    beside = jnp.broadcast_to(west_row >> 3, (8, lanes))
    west = east = north = south = top = bottom = satur = jnp.zeros((8, lanes), F32)
    for g in range(22):
        at = 8 * g
        face = found_ref[at : at + 8, :]
        west = jnp.where(beside == g, face, west)
        if g < 20:
            mask = here == g
            east = jnp.where(mask, face, east)
            north = jnp.where(mask, found_ref[NORTH + at : NORTH + at + 8, :], north)
            south = jnp.where(mask, found_ref[SOUTH + at : SOUTH + at + 8, :], south)
            satur = jnp.where(mask, found_ref[SATUR + at : SATUR + at + 8, :], satur)
            if g < 18:
                top = jnp.where(mask, found_ref[LEVEL + at : LEVEL + at + 8, :], top)
            if g >= 2:
                bottom = jnp.where(mask, found_ref[LEVEL + at - 16 : LEVEL + at - 8, :], bottom)
    row = index_of((8, lanes), 0)
    own = row == (high & 7)
    other = row == (west_row & 7)

    def pick(mask, rows):
        return jnp.sum(jnp.where(mask, rows, 0.0), axis=0, keepdims=True)

    return [pick(other, west)] + [pick(own, v) for v in (east, south, north, bottom, top, satur)]


def advance(record, sampled):
    west, east, south, north, bottom, top, satur = sampled
    scale = TIME_STEP / (POROSITY * satur)
    move_x = scale * (west + record[0:1] * (east - west))
    move_y = scale * (south + record[1:2] * (north - south))
    move_z = scale * (bottom + record[2:3] * (top - bottom))
    row = index_of(record.shape, 0)
    step = jnp.where(
        (row == 0) | (row == 6),
        move_x,
        jnp.where((row == 1) | (row == 7), move_y, jnp.where(row == 2, move_z, TIME_STEP)),
    )
    decayed = record * jnp.exp(-DECAY_RATE * TIME_STEP * satur)
    return jnp.where(row == 4, decayed, jnp.where(row == 5, satur, record + step))


def advance_group(tab_ref, cell_ref, rec_ref, found_ref, first, size, store):
    cells = jnp.concatenate([cell_ref[pl.ds(first + j, 1), :] for j in range(size)], axis=1)
    sampled = sample(tab_ref, cells, found_ref)
    for j in range(size):
        mine = [v[:, 128 * j : 128 * j + 128] for v in sampled]
        store(first + j, advance(rec_ref[first + j], mine))


def beside_lanes(tiles):
    lane = index_of(tiles[0].shape, 1)
    ahead = [roll(t, -1, 1) for t in tiles]
    back = [roll(t, 1, 1) for t in tiles]
    after = [jnp.where(lane == 127, ahead[(j + 1) % 3], ahead[j]) for j in range(3)]
    before = [jnp.where(lane == 0, back[(j + 2) % 3], back[j]) for j in range(3)]
    return after, before


def sweep_kernel(
    small_ref, p_ref, c_ref, s_ref, q_ref, rxe_ref, rxo_ref, rye_ref, ryo_ref, rec_ref, cell_ref,
    head_ref, tab_ref, kept, xe_ref, xo_ref, ye_ref, yo_ref,
    h0, h1, cond, wx, rhs, inv, wy, wy_back, wz, flat, found, sent, final, live_ref, sem,
):
    par_x, par_y = parities()
    edge = jnp.zeros((NZ, 3, 8, 128), F32)
    for ref in (h0, h1, cond, wx):
        ref[:, :, 0:8, :] = edge
        ref[:, :, 8 + ROWS : TALL, :] = edge
    east = jnp.where(par_x == 0, rxe_ref[...], rxo_ref[...])
    west = jnp.where(par_x == 0, rxo_ref[...], rxe_ref[...])
    north = [jnp.where(par_y == 0, rye_ref[j], ryo_ref[j]) for j in range(4)]
    south = [jnp.where(par_y == 0, ryo_ref[j], rye_ref[j]) for j in range(4)]
    lane = index_of((1, 128), 1)
    for f, (ref, base) in enumerate(((h0, 8), (cond, 8), (inv, 0), (rhs, 0))):
        for j in range(2):
            at = slice(128 * j, 128 * j + 128)
            own = (p_ref, c_ref, s_ref)[f][:, :, at] if f < 3 else s_ref[:, :, at] * p_ref[:, :, at] + q_ref[:, :, at]
            ref[:, j, base : base + 4, :] = west[:, 4 * f : 4 * f + 4, at]
            ref[:, j, base + 4 : base + 4 + CX, :] = own
            ref[:, j, base + 4 + CX : base + ROWS, :] = east[:, 4 * f : 4 * f + 4, at]
        for i in range(30):
            k, t = divmod(i, 3)
            slot = 8 * f + i % 8
            up = roll(north[i // 8], -4 * slot, 1)
            down = roll(south[i // 8], 124 - 4 * slot, 1)
            rows = jnp.where(lane < 4, up, jnp.where(lane >= 124, down, 0.0))
            if t < 2:
                ref[k, 2, base + 4 + 8 * t : base + 12 + 8 * t, :] = rows
            else:
                ref[k, 2, base + 4 + CX : base + ROWS, :] = rows[0:4]
                ref[k, 2, base : base + 4, :] = rows[4:8]
    for k in range(NZ):
        c = [cond[k, j, MID, :] for j in range(3)]
        after, _ = beside_lanes(c)
        w_y = [harmonic(c[j], after[j]) for j in range(3)]
        _, w_back = beside_lanes(w_y)
        for j in range(3):
            wx[k, j, MID, :] = harmonic(c[j], cond[k, j, 9 : 9 + ROWS, :])
            wy[k, j] = w_y[j]
            wy_back[k, j] = w_back[j]
            diag = inv[k, j] + wx[k, j, MID, :] + wx[k, j, 7 : 7 + ROWS, :] + w_y[j] + w_back[j]
            if k > 0:
                diag = diag + wz[k - 1, j]
            if k < NZ - 1:
                w_z = VERTICAL * harmonic(c[j], cond[k + 1, j, MID, :])
                wz[k, j] = w_z
                diag = diag + w_z
            inv[k, j] = OMEGA_RELAX / (diag + (diag == 0.0).astype(F32))
    old, new = h0, h1
    for _ in range(ITERS):
        for k in range(NZ):
            h = [old[k, j, MID, :] for j in range(3)]
            after, before = beside_lanes(h)
            for j in range(3):
                total = rhs[k, j]
                if k > 0:
                    total = total + wz[k - 1, j] * old[k - 1, j, MID, :]
                if k < NZ - 1:
                    total = total + wz[k, j] * old[k + 1, j, MID, :]
                along_x = wx[k, j, MID, :] * old[k, j, 9 : 9 + ROWS, :] + wx[k, j, 7 : 7 + ROWS, :] * old[k, j, 7 : 7 + ROWS, :]
                along_y = wy[k, j] * after[j] + wy_back[k, j] * before[j]
                new[k, j, MID, :] = (1.0 - OMEGA_RELAX) * h[j] + inv[k, j] * (along_x + along_y + total)
        old, new = new, old
    flat[NZ * CX : NORTH, :] = jnp.zeros((16, CY), F32)
    for k in range(NZ):
        h = [old[k, j, OWN, :] for j in range(3)]
        after, before = beside_lanes(h)
        at = slice(CX * k, CX * k + CX)
        for j in range(2):
            lanes = slice(128 * j, 128 * j + 128)

            def put(first, value):
                flat[first + CX * k : first + CX * k + CX, lanes] = value

            final[k, :, lanes] = h[j]
            put(EAST, -wx[k, j, OWN, :] * (old[k, j, 13 : 13 + CX, :] - h[j]))
            flat[NZ * CX + k : NZ * CX + k + 1, lanes] = -wx[k, j, 11:12, :] * (h[j][0:1] - old[k, j, 11:12, :])
            put(NORTH, -wy[k, j, INNER, :] * (after[j] - h[j]))
            put(SOUTH, -wy_back[k, j, INNER, :] * (h[j] - before[j]))
            if k < NZ - 1:
                put(LEVEL, -wz[k, j, INNER, :] * (old[k + 1, j, OWN, :] - h[j] + 1.0))
            suction = jnp.maximum(-h[j], 0.0)
            put(SATUR, RESIDUAL_SAT + (1.0 - RESIDUAL_SAT) * lax.rsqrt(1.0 + suction * suction))
    head_copy = pltpu.make_async_copy(final, head_ref, sem)
    head_copy.start()
    coarse, fine = split(flat[...], 2)
    tab_ref[:, 0:CY] = coarse
    tab_ref[:, CY : 2 * CY] = fine
    counts = small_ref[16:17, :]
    first = 0
    for d, cap in enumerate((CAPX, CAPX, CAPY, CAPY)):
        count = jnp.sum(jnp.where(lane == d, counts, 0), axis=1, keepdims=True)
        live_ref[first : first + cap, :] = (index_of((cap, 128), 0) < count).astype(F32)
        first += cap

    def store(slot, record):
        live = live_ref[pl.ds(slot, 1), :] > 0.0
        kept[slot] = jnp.where(live, 0.0, record)
        sent[slot] = jnp.where(live, record, 0.0)

    def group_step(i, carry):
        advance_group(tab_ref, cell_ref, rec_ref, found, i * GROUP_SENT, GROUP_SENT, store)
        return carry

    lax.fori_loop(0, SENT // GROUP_SENT, group_step, 0)
    links = jnp.concatenate([small_ref[j : j + 1, :] for j in range(8)], axis=1)
    surface = jnp.concatenate(split(final[NZ - 1], 3), axis=0)
    at_links = jnp.dot(surface, one_hot(links & (CY - 1), 1024), preferred_element_type=F32)
    at_links = at_links[0:CX] + at_links[CX : 2 * CX] + at_links[2 * CX : 3 * CX]
    picked = jnp.where(index_of((CX, 1024), 0) == (links >> 8), at_links, 0.0)
    value = jnp.sum(picked, axis=0, keepdims=True)
    flow = jnp.maximum(value, 0.0) + jnp.log1p(jnp.exp(-jnp.abs(value)))
    flows = [
        jnp.concatenate([flow[:, 256 * d : 256 * d + 128], flow[:, 256 * d + 128 : 256 * d + 256]] * 4, axis=0)
        for d in range(4)
    ]
    for ref, par, low, cap, within in (
        (xe_ref, par_x, 0, CAPX, None),
        (xo_ref, 1 - par_x, 0, CAPX, in_grid("gx")),
        (ye_ref, par_y, 2, CAPY, None),
        (yo_ref, 1 - par_y, 2, CAPY, in_grid("gy")),
    ):
        base = 2 * CAPX if low else 0
        leaving = sent[pl.ds(base + par * cap, cap)]
        flow_out = jnp.where(par == 0, flows[low], flows[low + 1])
        ref[0:cap] = leaving if within is None else jnp.where(within == 0, 0.0, leaving)
        ref[cap] = flow_out if within is None else jnp.where(within == 0, 0.0, flow_out)
    head_copy.wait()


def rest_kernel(first, size, tab_ref, rec_ref, cell_ref, *refs):
    kept, found = refs[-2:]

    def store(slot, record):
        kept[slot - first] = record

    advance_group(tab_ref, cell_ref, rec_ref, found, first, size, store)


def arrive_kernel(small_ref, xe_ref, xo_ref, ye_ref, yo_ref, *refs):
    kept = refs[:-3]
    next_ref, inflow_ref, sems = refs[-3:]
    par_x, par_y = parities()
    copies = []

    def send(source, first, count):
        copy = pltpu.make_async_copy(source, next_ref.at[pl.ds(first, count)], sems.at[len(copies)])
        copy.start()
        copies.append(copy)

    send(kept[0], 0, SENT)
    first = SENT
    for ref, size in zip(kept[1:], GROUPS_KEEP):
        send(ref, first, size)
        first += size
    for ref, par, base, cap in (
        (xe_ref, 1 - par_x, PB, CAPX),
        (xo_ref, par_x, PB, CAPX),
        (ye_ref, 1 - par_y, PB + 2 * CAPX, CAPY),
        (yo_ref, par_y, PB + 2 * CAPX, CAPY),
    ):
        send(ref.at[pl.ds(0, cap)], base + par * cap, cap)
    x_even, x_odd = xe_ref[CAPX], xo_ref[CAPX]
    y_even, y_odd = ye_ref[CAPY], yo_ref[CAPY]
    arrivals = [
        jnp.where(par_x == 0, x_odd, x_even),
        jnp.where(par_x == 0, x_even, x_odd),
        jnp.where(par_y == 0, y_odd, y_even),
        jnp.where(par_y == 0, y_even, y_odd),
    ]
    flow = jnp.concatenate([a[r : r + 1] for a in arrivals for r in range(2)], axis=1)
    links = jnp.concatenate([small_ref[j : j + 1, :] for j in range(8, 16)], axis=1)
    spread = jnp.where(index_of((CX, 1024), 0) == (links >> 8), flow, 0.0)
    parts = jnp.concatenate(split(spread, 3), axis=0)
    hot = one_hot(links & (CY - 1), 1024)
    total = lax.dot_general(parts, hot, (((1,), (1,)), ((), ())), preferred_element_type=F32)
    inflow_ref[...] = total[0:CX] + total[CX : 2 * CX] + total[2 * CX : 3 * CX]
    for copy in copies:
        copy.wait()


VMEM = pl.BlockSpec(memory_space=pltpu.VMEM)
ANY = pl.BlockSpec(memory_space=pl.ANY)
LIMIT = pltpu.CompilerParams(vmem_limit_bytes=32 << 20)


AXES = ("gx", "gy")


def swap(value, axis, first):
    sizes = [lax.axis_size(name) for name in AXES]
    along, across = AXES.index(axis), 1 - AXES.index(axis)

    def place(i, other):
        at = (i, other) if along == 0 else (other, i)
        return at[0] * sizes[1] + at[1]

    pairs = []
    for other in range(sizes[across]):
        for i in range(first, sizes[along] - 1, 2):
            pairs.append((place(i, other), place(i + 1, other)))
    if first:
        for end in (0, sizes[along] - 1):
            for other in range(0, sizes[across], 2):
                pairs.append((place(end, other), place(end, other + 1)))
    return lax.ppermute(value, AXES, pairs + [(b, a) for a, b in pairs])


def exchange(even, odd, axis):
    from_odd = swap(odd, axis, 1)
    from_even = swap(even, axis, 0)
    return from_even, from_odd


def shape(*dims, dtype=F32):
    return jax.ShapeDtypeStruct(dims, dtype)


def body(
    pressure, conductivity, storage, source, particles, crossing, particle_cell, river_source, river_target
):
    counts = jnp.pad(crossing.reshape(1, 4), ((0, 7), (0, 124)))
    small = jnp.concatenate([river_source.reshape(8, 128), river_target.reshape(8, 128), counts], axis=0)
    grid = (pressure, conductivity, storage, source)
    tile = pltpu.VMEM((NZ, CX, CY), F32)
    x_odd, *grid = pl.pallas_call(
        odd_rows_kernel,
        out_shape=(shape(NZ, CX, CY),) * 5,
        in_specs=[ANY] * 4,
        out_specs=(VMEM,) * 5,
        scratch_shapes=[pltpu.SemaphoreType.DMA((2, 4))],
        compiler_params=pltpu.CompilerParams(vmem_limit_bytes=54400 << 10),
        name="odd_rows",
    )(*grid)
    from_odd = swap(x_odd, "gx", 1)
    x_even = pl.pallas_call(
        even_rows_kernel,
        out_shape=shape(NZ, CX, CY),
        in_specs=[VMEM] * 4,
        out_specs=VMEM,
        compiler_params=LIMIT,
        name="even_rows",
    )(*grid)
    halo_x = (swap(x_even, "gx", 0), from_odd)
    y_even, y_odd = pl.pallas_call(
        edge_lanes_kernel,
        out_shape=(shape(4, 8, 128), shape(4, 8, 128)),
        in_specs=[VMEM] * 6,
        out_specs=(VMEM, VMEM),
        compiler_params=LIMIT,
        name="edge_lanes",
    )(*grid, *halo_x)
    halo_y = exchange(y_even, y_odd, "gy")
    records = particles[0, 0]
    cells = particle_cell[0, 0]
    tall = pltpu.VMEM((NZ, 3, TALL, 128), F32)
    field = pltpu.VMEM((NZ, 3, ROWS, 128), F32)
    head, table, kept, x_even, x_odd, y_even, y_odd = pl.pallas_call(
        sweep_kernel,
        out_shape=(
            shape(NZ, CX, CY),
            shape(TABLE, 2 * CY, dtype=BF16),
            shape(SENT, 8, 128),
            shape(CAPX + 1, 8, 128),
            shape(CAPX + 1, 8, 128),
            shape(CAPY + 1, 8, 128),
            shape(CAPY + 1, 8, 128),
        ),
        in_specs=[VMEM] * 11,
        out_specs=(ANY,) + (VMEM,) * 6,
        scratch_shapes=[tall] * 4
        + [field] * 5
        + [
            pltpu.VMEM((TABLE, CY), F32),
            pltpu.VMEM((TABLE, 128 * GROUP_SENT), F32),
            pltpu.VMEM((SENT, 8, 128), F32),
            tile,
            pltpu.VMEM((SENT, 128), F32),
            pltpu.SemaphoreType.DMA,
        ],
        compiler_params=LIMIT,
        name="sweep",
    )(small, *grid, *halo_x, *halo_y, records, cells)
    stages = (
        (("x_odd", "gx", 1),),
        (("y_even", "gy", 0),),
        (("y_odd", "gy", 1), ("x_even", "gx", 0)),
    )
    waiting = {"x_odd": x_odd, "y_even": y_even, "y_odd": y_odd, "x_even": x_even}
    received = {}
    done = [kept]
    first = SENT
    for n, stage in enumerate(stages):
        for name, axis, parity in stage:
            received[name] = swap(waiting[name], axis, parity)
        later = [name for name, _, _ in stages[n + 1]] if n + 1 < len(stages) else []
        size = GROUPS_KEEP[n]
        outs = pl.pallas_call(
            functools.partial(rest_kernel, first, size),
            out_shape=[jax.ShapeDtypeStruct(waiting[v].shape, F32) for v in later] + [shape(size, 8, 128)],
            in_specs=[VMEM] * (3 + len(later)),
            out_specs=[VMEM] * (1 + len(later)),
            scratch_shapes=[pltpu.VMEM((TABLE, 128 * size), F32)],
            input_output_aliases={3 + i: i for i in range(len(later))},
            compiler_params=LIMIT,
            cost_estimate=pl.CostEstimate(
                flops=2 * TABLE * 512 * 128 * size, bytes_accessed=1 << 20, transcendentals=0
            ),
            name=f"rest_{n}",
        )(table, records, cells, *(waiting[v] for v in later))
        done.append(outs[-1])
        waiting.update(zip(later, outs))
        first += size
    moved, inflow = pl.pallas_call(
        arrive_kernel,
        out_shape=(shape(OUT, 8, 128), shape(CX, CY)),
        in_specs=[VMEM] * (5 + len(done)),
        out_specs=(ANY, VMEM),
        scratch_shapes=[pltpu.SemaphoreType.DMA((4 + len(done),))],
        compiler_params=LIMIT,
        name="arrive",
    )(small, *(received[v] for v in ("x_even", "x_odd", "y_even", "y_odd")), *done)
    return head, moved[None, None], inflow


def solution(mesh):
    in_specs = (
        P(None, "gx", "gy"),
        P(None, "gx", "gy"),
        P(None, "gx", "gy"),
        P(None, "gx", "gy"),
        P("gx", "gy", None, None, None),
        P("gx", "gy", None),
        P("gx", "gy", None, None),
        P("gx", "gy", None, None, None),
        P("gx", "gy", None, None, None),
    )
    out_specs = (P(None, "gx", "gy"), P("gx", "gy", None, None, None), P("gx", "gy"))
    return jax.shard_map(body, mesh=mesh, in_specs=in_specs, out_specs=out_specs, check_vma=False)
```

```python
import functools

import jax
import jax.numpy as jnp
from jax import lax
from jax.experimental import pallas as pl
from jax.experimental.pallas import tpu as pltpu
from jax.sharding import PartitionSpec as P

F32 = jnp.float32
BF16 = jnp.bfloat16
F8 = jnp.float8_e4m3fn

ITERS = 4
CAPX = 16
CAPY = 4
NZ = 10
CX = 16
CY = 256
PB = 104
SENT = 2 * CAPX + 2 * CAPY
KEEP = PB - SENT
OUT = PB + SENT
GROUP_SENT = 40
GROUPS_KEEP = (64,)

OMEGA_RELAX = 0.8
VERTICAL = 4.0
POROSITY = 0.4
RESIDUAL_SAT = 0.1
TIME_STEP = 0.01
DECAY_RATE = 20.0

ROWS = CX + 8
TALL = 8 + ROWS + 8
MID = slice(8, 8 + ROWS)
OWN = slice(12, 12 + CX)
INNER = slice(4, 4 + CX)

EAST = 0
NORTH = 176
SOUTH = 336
LEVEL = 496
SATUR = 640
TABLE = 800

PARTS = 3
STEP_DOWN = 0.0625
SIDE_SCALE = 0.5
LEVEL_SCALE = 0.125
SATUR_SCALE = 256.0


def harmonic(left, right):
    total = left + right
    return 2.0 * left * right / (total + (total == 0.0).astype(total.dtype))


def index_of(shape, axis):
    return lax.broadcasted_iota(jnp.int32, shape, axis)


def roll(x, shift, axis):
    return pltpu.roll(x, shift % x.shape[axis], axis)


def in_grid(axis):
    here = lax.axis_index(axis)
    return jnp.where((here == 0) | (here == lax.axis_size(axis) - 1), 0, 1)


def parities():
    return lax.rem(lax.axis_index("gx"), 2), lax.rem(lax.axis_index("gy"), 2)


def edge_of(p, c, s, q, low):
    step, outer = (-1, 3) if low else (1, 4)
    weight = jnp.where(index_of((1, 8, CY), 1) == outer, harmonic(c, roll(c, step, 1)), 0.0)
    rhs = s * p + q + weight * roll(p, step, 1)
    side = slice(0, 4) if low else slice(4, 8)
    return jnp.concatenate([p[:, side], c[:, side], (s + weight)[:, side], rhs[:, side]], axis=1)


def odd_rows_kernel(p_hbm, c_hbm, s_hbm, q_hbm, odd_ref, p_ref, c_ref, s_ref, q_ref, sems):
    parity = parities()[0]
    within = in_grid("gx")
    pairs = ((p_hbm, p_ref), (c_hbm, c_ref), (s_hbm, s_ref), (q_hbm, q_ref))
    loads = []
    for h, tile in enumerate((parity, 1 - parity)):
        rows = pl.ds(pl.multiple_of(8 * tile, 8), 8)
        for n, (source, ref) in enumerate(pairs):
            copy = pltpu.make_async_copy(source.at[:, rows, :], ref.at[:, rows, :], sems.at[h, n])
            copy.start()
            loads.append(copy)
    for copy in loads[:4]:
        copy.wait()
    rows = pl.ds(pl.multiple_of(8 * parity, 8), 8)
    fields = [ref[:, rows, :] for _, ref in pairs]
    edge = jnp.where(parity == 0, edge_of(*fields, True), edge_of(*fields, False))
    odd_ref[...] = jnp.where(within == 0, 0.0, edge)
    for copy in loads[4:]:
        copy.wait()


def even_rows_kernel(p_ref, c_ref, s_ref, q_ref, even_ref):
    parity = parities()[0]
    refs = (p_ref, c_ref, s_ref, q_ref)
    west = edge_of(*(ref[:, 0:8, :] for ref in refs), True)
    east = edge_of(*(ref[:, 8:16, :] for ref in refs), False)
    even_ref[...] = jnp.where(parity == 0, east, west)


def beside_rows(from_even, from_odd, par_x):
    east = jnp.where(par_x == 0, from_even, from_odd)
    west = jnp.where(par_x == 0, from_odd, from_even)
    return [jnp.concatenate([east[:, 4 * f : 4 * f + 4], west[:, 4 * f : 4 * f + 4]], axis=1) for f in range(4)]


def edge_lanes_kernel(p_ref, c_ref, s_ref, q_ref, re_ref, ro_ref, even_ref, odd_ref):
    par_x, par_y = parities()
    lane = index_of((1, 1, 128), 2)
    packed = []
    for start, step, outer, low in ((0, -1, 3, 0), (128, 1, 124, 124)):
        at = slice(start, start + 128)
        near = beside_rows(re_ref[:, :, at], ro_ref[:, :, at], par_x)
        p, c, s, q = (ref[:, :, at] for ref in (p_ref, c_ref, s_ref, q_ref))
        p, c, s, r = (jnp.concatenate(pair, axis=1) for pair in zip((p, c, s, s * p + q), near))
        weight = jnp.where(lane == outer, harmonic(c, roll(c, step, 2)), 0.0)
        fields = [p, c, s + weight, r + weight * roll(p, step, 2)]
        inside = (lane >= low) & (lane < low + 4)
        total = [jnp.zeros((8, 128), F32) for _ in range(4)]
        for f in range(4):
            rows = jnp.where(inside, fields[f], 0.0).reshape(30, 8, 128)
            for i in range(30):
                slot = 8 * f + i % 8
                total[i // 8] = total[i // 8] + roll(rows[i], 4 * slot - low, 1)
        packed.append(total)
    south, north = packed
    within = in_grid("gy")
    for j in range(4):
        even_ref[j] = jnp.where(par_y == 0, north[j], south[j])
        odd_ref[j] = jnp.where(within == 0, 0.0, jnp.where(par_y == 0, south[j], north[j]))


def one_hot(values, lanes):
    hit = index_of((CY, lanes), 0).astype(BF16) == values.astype(BF16)
    return jnp.where(hit, jnp.ones((), BF16), jnp.zeros((), BF16))


def split(x, parts):
    out = []
    for _ in range(parts):
        piece = x.astype(BF16)
        out.append(piece)
        x = x - piece.astype(F32)
    return out


def sample(tab_ref, cells, found_ref):
    lanes = cells.shape[1]
    hot = one_hot(cells & (CY - 1), lanes)
    hot = jnp.concatenate([(hot * jnp.asarray(STEP_DOWN**n, BF16)).astype(F8) for n in range(PARTS)], axis=0)
    found_ref[...] = jnp.dot(tab_ref[...], hot, preferred_element_type=F32)
    high = cells >> 8
    column = high & (CX - 1)
    west_row = jnp.where(column == 0, NZ * CX + (high >> 4), high - 1)
    here = jnp.broadcast_to(high >> 3, (8, lanes))
    beside = jnp.broadcast_to(west_row >> 3, (8, lanes))
    west = east = north = south = top = bottom = satur = jnp.zeros((8, lanes), F32)
    for g in range(22):
        at = 8 * g
        face = found_ref[at : at + 8, :]
        west = jnp.where(beside == g, face, west)
        if g < 20:
            mask = here == g
            east = jnp.where(mask, face, east)
            north = jnp.where(mask, found_ref[NORTH + at : NORTH + at + 8, :], north)
            south = jnp.where(mask, found_ref[SOUTH + at : SOUTH + at + 8, :], south)
            satur = jnp.where(mask, found_ref[SATUR + at : SATUR + at + 8, :], satur)
            if g < 18:
                top = jnp.where(mask, found_ref[LEVEL + at : LEVEL + at + 8, :], top)
            if g >= 2:
                bottom = jnp.where(mask, found_ref[LEVEL + at - 16 : LEVEL + at - 8, :], bottom)
    row = index_of((8, lanes), 0)
    own = row == (high & 7)
    other = row == (west_row & 7)

    def pick(mask, rows):
        return jnp.sum(jnp.where(mask, rows, 0.0), axis=0, keepdims=True)

    values = [(other, west), (own, east), (own, south), (own, north), (own, bottom), (own, top), (own, satur)]
    scales = [SIDE_SCALE] * 4 + [LEVEL_SCALE] * 2 + [SATUR_SCALE]
    return [pick(mask, v) * (1.0 / scale) for (mask, v), scale in zip(values, scales)]


def advance(record, sampled):
    west, east, south, north, bottom, top, satur = sampled
    scale = TIME_STEP / (POROSITY * satur)
    move_x = scale * (west + record[0:1] * (east - west))
    move_y = scale * (south + record[1:2] * (north - south))
    move_z = scale * (bottom + record[2:3] * (top - bottom))
    row = index_of(record.shape, 0)
    step = jnp.where(
        (row == 0) | (row == 6),
        move_x,
        jnp.where((row == 1) | (row == 7), move_y, jnp.where(row == 2, move_z, TIME_STEP)),
    )
    decayed = record * jnp.exp(-DECAY_RATE * TIME_STEP * satur)
    return jnp.where(row == 4, decayed, jnp.where(row == 5, satur, record + step))


def advance_group(tab_ref, cell_ref, rec_ref, found_ref, first, size, store):
    cells = jnp.concatenate([cell_ref[pl.ds(first + j, 1), :] for j in range(size)], axis=1)
    sampled = sample(tab_ref, cells, found_ref)
    for j in range(size):
        mine = [v[:, 128 * j : 128 * j + 128] for v in sampled]
        store(first + j, advance(rec_ref[first + j], mine))


def beside_lanes(tiles):
    lane = index_of(tiles[0].shape, 1)
    ahead = [roll(t, -1, 1) for t in tiles]
    back = [roll(t, 1, 1) for t in tiles]
    after = [jnp.where(lane == 127, ahead[(j + 1) % 3], ahead[j]) for j in range(3)]
    before = [jnp.where(lane == 0, back[(j + 2) % 3], back[j]) for j in range(3)]
    return after, before


def sweep_kernel(
    small_ref, p_ref, c_ref, s_ref, q_ref, rxe_ref, rxo_ref, rye_ref, ryo_ref, rec_ref, cell_ref,
    head_ref, tab_ref, kept, xe_ref, xo_ref, ye_ref, yo_ref,
    h0, h1, cond, wx, rhs, inv, wy, wy_back, wz, flat, found, sent, final, live_ref, sem,
):
    par_x, par_y = parities()
    edge = jnp.zeros((NZ, 3, 8, 128), F32)
    for ref in (h0, h1, cond, wx):
        ref[:, :, 0:8, :] = edge
        ref[:, :, 8 + ROWS : TALL, :] = edge
    east = jnp.where(par_x == 0, rxe_ref[...], rxo_ref[...])
    west = jnp.where(par_x == 0, rxo_ref[...], rxe_ref[...])
    north = [jnp.where(par_y == 0, rye_ref[j], ryo_ref[j]) for j in range(4)]
    south = [jnp.where(par_y == 0, ryo_ref[j], rye_ref[j]) for j in range(4)]
    lane = index_of((1, 128), 1)
    for f, (ref, base) in enumerate(((h0, 8), (cond, 8), (inv, 0), (rhs, 0))):
        for j in range(2):
            at = slice(128 * j, 128 * j + 128)
            own = (p_ref, c_ref, s_ref)[f][:, :, at] if f < 3 else s_ref[:, :, at] * p_ref[:, :, at] + q_ref[:, :, at]
            ref[:, j, base : base + 4, :] = west[:, 4 * f : 4 * f + 4, at]
            ref[:, j, base + 4 : base + 4 + CX, :] = own
            ref[:, j, base + 4 + CX : base + ROWS, :] = east[:, 4 * f : 4 * f + 4, at]
        for i in range(30):
            k, t = divmod(i, 3)
            slot = 8 * f + i % 8
            up = roll(north[i // 8], -4 * slot, 1)
            down = roll(south[i // 8], 124 - 4 * slot, 1)
            rows = jnp.where(lane < 4, up, jnp.where(lane >= 124, down, 0.0))
            if t < 2:
                ref[k, 2, base + 4 + 8 * t : base + 12 + 8 * t, :] = rows
            else:
                ref[k, 2, base + 4 + CX : base + ROWS, :] = rows[0:4]
                ref[k, 2, base : base + 4, :] = rows[4:8]
    for k in range(NZ):
        c = [cond[k, j, MID, :] for j in range(3)]
        after, _ = beside_lanes(c)
        w_y = [harmonic(c[j], after[j]) for j in range(3)]
        _, w_back = beside_lanes(w_y)
        for j in range(3):
            wx[k, j, MID, :] = harmonic(c[j], cond[k, j, 9 : 9 + ROWS, :])
            wy[k, j] = w_y[j]
            wy_back[k, j] = w_back[j]
            diag = inv[k, j] + wx[k, j, MID, :] + wx[k, j, 7 : 7 + ROWS, :] + w_y[j] + w_back[j]
            if k > 0:
                diag = diag + wz[k - 1, j]
            if k < NZ - 1:
                w_z = VERTICAL * harmonic(c[j], cond[k + 1, j, MID, :])
                wz[k, j] = w_z
                diag = diag + w_z
            inv[k, j] = OMEGA_RELAX / (diag + (diag == 0.0).astype(F32))
    old, new = h0, h1
    for _ in range(ITERS):
        for k in range(NZ):
            h = [old[k, j, MID, :] for j in range(3)]
            after, before = beside_lanes(h)
            for j in range(3):
                total = rhs[k, j]
                if k > 0:
                    total = total + wz[k - 1, j] * old[k - 1, j, MID, :]
                if k < NZ - 1:
                    total = total + wz[k, j] * old[k + 1, j, MID, :]
                along_x = wx[k, j, MID, :] * old[k, j, 9 : 9 + ROWS, :] + wx[k, j, 7 : 7 + ROWS, :] * old[k, j, 7 : 7 + ROWS, :]
                along_y = wy[k, j] * after[j] + wy_back[k, j] * before[j]
                new[k, j, MID, :] = (1.0 - OMEGA_RELAX) * h[j] + inv[k, j] * (along_x + along_y + total)
        old, new = new, old
    flat[NZ * CX : NORTH, :] = jnp.zeros((16, CY), F32)
    for k in range(NZ):
        h = [old[k, j, OWN, :] for j in range(3)]
        after, before = beside_lanes(h)
        at = slice(CX * k, CX * k + CX)
        for j in range(2):
            lanes = slice(128 * j, 128 * j + 128)

            def put(first, value):
                flat[first + CX * k : first + CX * k + CX, lanes] = value

            final[k, :, lanes] = h[j]
            put(EAST, -SIDE_SCALE * wx[k, j, OWN, :] * (old[k, j, 13 : 13 + CX, :] - h[j]))
            flat[NZ * CX + k : NZ * CX + k + 1, lanes] = -SIDE_SCALE * wx[k, j, 11:12, :] * (h[j][0:1] - old[k, j, 11:12, :])
            put(NORTH, -SIDE_SCALE * wy[k, j, INNER, :] * (after[j] - h[j]))
            put(SOUTH, -SIDE_SCALE * wy_back[k, j, INNER, :] * (h[j] - before[j]))
            if k < NZ - 1:
                put(LEVEL, -LEVEL_SCALE * wz[k, j, INNER, :] * (old[k + 1, j, OWN, :] - h[j] + 1.0))
            suction = jnp.maximum(-h[j], 0.0)
            put(SATUR, SATUR_SCALE * (RESIDUAL_SAT + (1.0 - RESIDUAL_SAT) * lax.rsqrt(1.0 + suction * suction)))
    head_copy = pltpu.make_async_copy(final, head_ref, sem)
    head_copy.start()
    rest = flat[...]
    for n in range(PARTS):
        piece = rest.astype(F8)
        tab_ref[:, CY * n : CY * n + CY] = piece
        rest = (rest - piece.astype(F32)) * (1.0 / STEP_DOWN)
    counts = small_ref[16:17, :]
    first = 0
    for d, cap in enumerate((CAPX, CAPX, CAPY, CAPY)):
        count = jnp.sum(jnp.where(lane == d, counts, 0), axis=1, keepdims=True)
        live_ref[first : first + cap, :] = (index_of((cap, 128), 0) < count).astype(F32)
        first += cap

    def store(slot, record):
        live = live_ref[pl.ds(slot, 1), :] > 0.0
        kept[slot] = jnp.where(live, 0.0, record)
        sent[slot] = jnp.where(live, record, 0.0)

    def group_step(i, carry):
        advance_group(tab_ref, cell_ref, rec_ref, found, i * GROUP_SENT, GROUP_SENT, store)
        return carry

    lax.fori_loop(0, SENT // GROUP_SENT, group_step, 0)
    links = jnp.concatenate([small_ref[j : j + 1, :] for j in range(8)], axis=1)
    surface = jnp.concatenate(split(final[NZ - 1], 3), axis=0)
    at_links = jnp.dot(surface, one_hot(links & (CY - 1), 1024), preferred_element_type=F32)
    at_links = at_links[0:CX] + at_links[CX : 2 * CX] + at_links[2 * CX : 3 * CX]
    picked = jnp.where(index_of((CX, 1024), 0) == (links >> 8), at_links, 0.0)
    value = jnp.sum(picked, axis=0, keepdims=True)
    flow = jnp.maximum(value, 0.0) + jnp.log1p(jnp.exp(-jnp.abs(value)))
    flows = [
        jnp.concatenate([flow[:, 256 * d : 256 * d + 128], flow[:, 256 * d + 128 : 256 * d + 256]] * 4, axis=0)
        for d in range(4)
    ]
    for ref, par, low, cap, within in (
        (xe_ref, par_x, 0, CAPX, None),
        (xo_ref, 1 - par_x, 0, CAPX, in_grid("gx")),
        (ye_ref, par_y, 2, CAPY, None),
        (yo_ref, 1 - par_y, 2, CAPY, in_grid("gy")),
    ):
        base = 2 * CAPX if low else 0
        leaving = sent[pl.ds(base + par * cap, cap)]
        flow_out = jnp.where(par == 0, flows[low], flows[low + 1])
        ref[0:cap] = leaving if within is None else jnp.where(within == 0, 0.0, leaving)
        ref[cap] = flow_out if within is None else jnp.where(within == 0, 0.0, flow_out)
    head_copy.wait()


def rest_kernel(first, size, tab_ref, rec_ref, cell_ref, *refs):
    kept, found = refs[-2:]

    def store(slot, record):
        kept[slot - first] = record

    advance_group(tab_ref, cell_ref, rec_ref, found, first, size, store)


def arrive_kernel(small_ref, xe_ref, xo_ref, ye_ref, yo_ref, *refs):
    kept = refs[:-3]
    next_ref, inflow_ref, sems = refs[-3:]
    par_x, par_y = parities()
    copies = []

    def send(source, first, count):
        copy = pltpu.make_async_copy(source, next_ref.at[pl.ds(first, count)], sems.at[len(copies)])
        copy.start()
        copies.append(copy)

    send(kept[0], 0, SENT)
    first = SENT
    for ref, size in zip(kept[1:], GROUPS_KEEP):
        send(ref, first, size)
        first += size
    for ref, par, base, cap in (
        (xe_ref, 1 - par_x, PB, CAPX),
        (xo_ref, par_x, PB, CAPX),
        (ye_ref, 1 - par_y, PB + 2 * CAPX, CAPY),
        (yo_ref, par_y, PB + 2 * CAPX, CAPY),
    ):
        send(ref.at[pl.ds(0, cap)], base + par * cap, cap)
    x_even, x_odd = xe_ref[CAPX], xo_ref[CAPX]
    y_even, y_odd = ye_ref[CAPY], yo_ref[CAPY]
    arrivals = [
        jnp.where(par_x == 0, x_odd, x_even),
        jnp.where(par_x == 0, x_even, x_odd),
        jnp.where(par_y == 0, y_odd, y_even),
        jnp.where(par_y == 0, y_even, y_odd),
    ]
    flow = jnp.concatenate([a[r : r + 1] for a in arrivals for r in range(2)], axis=1)
    links = jnp.concatenate([small_ref[j : j + 1, :] for j in range(8, 16)], axis=1)
    spread = jnp.where(index_of((CX, 1024), 0) == (links >> 8), flow, 0.0)
    parts = jnp.concatenate(split(spread, 3), axis=0)
    hot = one_hot(links & (CY - 1), 1024)
    total = lax.dot_general(parts, hot, (((1,), (1,)), ((), ())), preferred_element_type=F32)
    inflow_ref[...] = total[0:CX] + total[CX : 2 * CX] + total[2 * CX : 3 * CX]
    for copy in copies:
        copy.wait()


VMEM = pl.BlockSpec(memory_space=pltpu.VMEM)
ANY = pl.BlockSpec(memory_space=pl.ANY)
LIMIT = pltpu.CompilerParams(vmem_limit_bytes=44 << 20)


AXES = ("gx", "gy")


def swap(value, axis, first):
    sizes = [lax.axis_size(name) for name in AXES]
    along, across = AXES.index(axis), 1 - AXES.index(axis)

    def place(i, other):
        at = (i, other) if along == 0 else (other, i)
        return at[0] * sizes[1] + at[1]

    pairs = []
    for other in range(sizes[across]):
        for i in range(first, sizes[along] - 1, 2):
            pairs.append((place(i, other), place(i + 1, other)))
    if first:
        for end in (0, sizes[along] - 1):
            for other in range(0, sizes[across], 2):
                pairs.append((place(end, other), place(end, other + 1)))
    return lax.ppermute(value, AXES, pairs + [(b, a) for a, b in pairs])


def exchange(even, odd, axis):
    from_odd = swap(odd, axis, 1)
    from_even = swap(even, axis, 0)
    return from_even, from_odd


def shape(*dims, dtype=F32):
    return jax.ShapeDtypeStruct(dims, dtype)


def body(
    pressure, conductivity, storage, source, particles, crossing, particle_cell, river_source, river_target
):
    counts = jnp.pad(crossing.reshape(1, 4), ((0, 7), (0, 124)))
    small = jnp.concatenate([river_source.reshape(8, 128), river_target.reshape(8, 128), counts], axis=0)
    grid = (pressure, conductivity, storage, source)
    tile = pltpu.VMEM((NZ, CX, CY), F32)
    x_odd, *grid = pl.pallas_call(
        odd_rows_kernel,
        out_shape=(shape(NZ, CX, CY),) * 5,
        in_specs=[ANY] * 4,
        out_specs=(VMEM,) * 5,
        scratch_shapes=[pltpu.SemaphoreType.DMA((2, 4))],
        compiler_params=pltpu.CompilerParams(vmem_limit_bytes=54400 << 10),
        name="odd_rows",
    )(*grid)
    from_odd = swap(x_odd, "gx", 1)
    x_even = pl.pallas_call(
        even_rows_kernel,
        out_shape=shape(NZ, CX, CY),
        in_specs=[VMEM] * 4,
        out_specs=VMEM,
        compiler_params=LIMIT,
        name="even_rows",
    )(*grid)
    halo_x = (swap(x_even, "gx", 0), from_odd)
    y_even, y_odd = pl.pallas_call(
        edge_lanes_kernel,
        out_shape=(shape(4, 8, 128), shape(4, 8, 128)),
        in_specs=[VMEM] * 6,
        out_specs=(VMEM, VMEM),
        compiler_params=LIMIT,
        name="edge_lanes",
    )(*grid, *halo_x)
    halo_y = exchange(y_even, y_odd, "gy")
    records = particles[0, 0]
    cells = particle_cell[0, 0]
    tall = pltpu.VMEM((NZ, 3, TALL, 128), F32)
    field = pltpu.VMEM((NZ, 3, ROWS, 128), F32)
    head, table, kept, x_even, x_odd, y_even, y_odd = pl.pallas_call(
        sweep_kernel,
        out_shape=(
            shape(NZ, CX, CY),
            shape(TABLE, PARTS * CY, dtype=F8),
            shape(SENT, 8, 128),
            shape(CAPX + 1, 8, 128),
            shape(CAPX + 1, 8, 128),
            shape(CAPY + 1, 8, 128),
            shape(CAPY + 1, 8, 128),
        ),
        in_specs=[VMEM] * 11,
        out_specs=(ANY,) + (VMEM,) * 6,
        scratch_shapes=[tall] * 4
        + [field] * 5
        + [
            pltpu.VMEM((TABLE, CY), F32),
            pltpu.VMEM((TABLE, 128 * GROUP_SENT), F32),
            pltpu.VMEM((SENT, 8, 128), F32),
            tile,
            pltpu.VMEM((SENT, 128), F32),
            pltpu.SemaphoreType.DMA,
        ],
        compiler_params=LIMIT,
        name="sweep",
    )(small, *grid, *halo_x, *halo_y, records, cells)
    stages = ((("x_odd", "gx", 1), ("y_even", "gy", 0), ("y_odd", "gy", 1), ("x_even", "gx", 0)),)
    waiting = {"x_odd": x_odd, "y_even": y_even, "y_odd": y_odd, "x_even": x_even}
    received = {}
    done = [kept]
    first = SENT
    for n, stage in enumerate(stages):
        for name, axis, parity in stage:
            received[name] = swap(waiting[name], axis, parity)
        later = [name for name, _, _ in stages[n + 1]] if n + 1 < len(stages) else []
        size = GROUPS_KEEP[n]
        outs = pl.pallas_call(
            functools.partial(rest_kernel, first, size),
            out_shape=[jax.ShapeDtypeStruct(waiting[v].shape, F32) for v in later] + [shape(size, 8, 128)],
            in_specs=[VMEM] * (3 + len(later)),
            out_specs=[VMEM] * (1 + len(later)),
            scratch_shapes=[pltpu.VMEM((TABLE, 128 * size), F32)],
            input_output_aliases={3 + i: i for i in range(len(later))},
            compiler_params=LIMIT,
            cost_estimate=pl.CostEstimate(
                flops=2 * TABLE * 512 * 128 * size, bytes_accessed=1 << 20, transcendentals=0
            ),
            name=f"rest_{n}",
        )(table, records, cells, *(waiting[v] for v in later))
        done.append(outs[-1])
        waiting.update(zip(later, outs))
        first += size
    moved, inflow = pl.pallas_call(
        arrive_kernel,
        out_shape=(shape(OUT, 8, 128), shape(CX, CY)),
        in_specs=[VMEM] * (5 + len(done)),
        out_specs=(ANY, VMEM),
        scratch_shapes=[pltpu.SemaphoreType.DMA((4 + len(done),))],
        compiler_params=LIMIT,
        name="arrive",
    )(small, *(received[v] for v in ("x_even", "x_odd", "y_even", "y_odd")), *done)
    return head, moved[None, None], inflow


def solution(mesh):
    in_specs = (
        P(None, "gx", "gy"),
        P(None, "gx", "gy"),
        P(None, "gx", "gy"),
        P(None, "gx", "gy"),
        P("gx", "gy", None, None, None),
        P("gx", "gy", None),
        P("gx", "gy", None, None),
        P("gx", "gy", None, None, None),
        P("gx", "gy", None, None, None),
    )
    out_specs = (P(None, "gx", "gy"), P("gx", "gy", None, None, None), P("gx", "gy"))
    return jax.shard_map(body, mesh=mesh, in_specs=in_specs, out_specs=out_specs, check_vma=False)
```

```python
import functools

import jax
import jax.numpy as jnp
from jax import lax
from jax.experimental import pallas as pl
from jax.experimental.pallas import tpu as pltpu
from jax.sharding import PartitionSpec as P

F32 = jnp.float32
BF16 = jnp.bfloat16
F8 = jnp.float8_e4m3fn

ITERS = 4
CAPX = 16
CAPY = 4
NZ = 10
CX = 16
CY = 256
PB = 104
SENT = 2 * CAPX + 2 * CAPY
KEEP = PB - SENT
OUT = PB + SENT
GROUP_SENT = 40
GROUPS_KEEP = (64,)

OMEGA_RELAX = 0.8
VERTICAL = 4.0
POROSITY = 0.4
RESIDUAL_SAT = 0.1
TIME_STEP = 0.01
DECAY_RATE = 20.0

ROWS = CX + 8
TALL = 8 + ROWS + 8
MID = slice(8, 8 + ROWS)
OWN = slice(12, 12 + CX)
INNER = slice(4, 4 + CX)

EAST = 0
NORTH = 176
SOUTH = 336
LEVEL = 496
SATUR = 640
TABLE = 800

PARTS = 3
STEP_DOWN = 0.0625
SIDE_SCALE = 0.5
LEVEL_SCALE = 0.125
SATUR_SCALE = 256.0


def harmonic(left, right):
    total = left + right
    return 2.0 * left * right / (total + (total == 0.0).astype(total.dtype))


def index_of(shape, axis):
    return lax.broadcasted_iota(jnp.int32, shape, axis)


def roll(x, shift, axis):
    return pltpu.roll(x, shift % x.shape[axis], axis)


def in_grid(axis):
    here = lax.axis_index(axis)
    return jnp.where((here == 0) | (here == lax.axis_size(axis) - 1), 0, 1)


def parities():
    return lax.rem(lax.axis_index("gx"), 2), lax.rem(lax.axis_index("gy"), 2)


def edge_of(p, c, s, q, low):
    step, outer = (-1, 3) if low else (1, 4)
    weight = jnp.where(index_of((1, 8, CY), 1) == outer, harmonic(c, roll(c, step, 1)), 0.0)
    rhs = s * p + q + weight * roll(p, step, 1)
    side = slice(0, 4) if low else slice(4, 8)
    return jnp.concatenate([p[:, side], c[:, side], (s + weight)[:, side], rhs[:, side]], axis=1)


def odd_rows_kernel(p_hbm, c_hbm, s_hbm, q_hbm, odd_ref, p_ref, c_ref, s_ref, q_ref, sems):
    parity = parities()[0]
    within = in_grid("gx")
    pairs = ((p_hbm, p_ref), (c_hbm, c_ref), (s_hbm, s_ref), (q_hbm, q_ref))
    loads = []
    for h, tile in enumerate((parity, 1 - parity)):
        rows = pl.ds(pl.multiple_of(8 * tile, 8), 8)
        for n, (source, ref) in enumerate(pairs):
            copy = pltpu.make_async_copy(source.at[:, rows, :], ref.at[:, rows, :], sems.at[h, n])
            copy.start()
            loads.append(copy)
    for copy in loads[:4]:
        copy.wait()
    rows = pl.ds(pl.multiple_of(8 * parity, 8), 8)
    fields = [ref[:, rows, :] for _, ref in pairs]
    edge = jnp.where(parity == 0, edge_of(*fields, True), edge_of(*fields, False))
    odd_ref[...] = jnp.where(within == 0, 0.0, edge)
    for copy in loads[4:]:
        copy.wait()


def even_rows_kernel(p_ref, c_ref, s_ref, q_ref, even_ref):
    parity = parities()[0]
    refs = (p_ref, c_ref, s_ref, q_ref)
    west = edge_of(*(ref[:, 0:8, :] for ref in refs), True)
    east = edge_of(*(ref[:, 8:16, :] for ref in refs), False)
    even_ref[...] = jnp.where(parity == 0, east, west)


def beside_rows(from_even, from_odd, par_x):
    east = jnp.where(par_x == 0, from_even, from_odd)
    west = jnp.where(par_x == 0, from_odd, from_even)
    return [jnp.concatenate([east[:, 4 * f : 4 * f + 4], west[:, 4 * f : 4 * f + 4]], axis=1) for f in range(4)]


def edge_lanes_kernel(p_ref, c_ref, s_ref, q_ref, re_ref, ro_ref, even_ref, odd_ref):
    par_x, par_y = parities()
    lane = index_of((1, 1, 128), 2)
    packed = []
    for start, step, outer, low in ((0, -1, 3, 0), (128, 1, 124, 124)):
        at = slice(start, start + 128)
        near = beside_rows(re_ref[:, :, at], ro_ref[:, :, at], par_x)
        p, c, s, q = (ref[:, :, at] for ref in (p_ref, c_ref, s_ref, q_ref))
        p, c, s, r = (jnp.concatenate(pair, axis=1) for pair in zip((p, c, s, s * p + q), near))
        weight = jnp.where(lane == outer, harmonic(c, roll(c, step, 2)), 0.0)
        fields = [p, c, s + weight, r + weight * roll(p, step, 2)]
        inside = (lane >= low) & (lane < low + 4)
        total = [jnp.zeros((8, 128), F32) for _ in range(4)]
        for f in range(4):
            rows = jnp.where(inside, fields[f], 0.0).reshape(30, 8, 128)
            for i in range(30):
                slot = 8 * f + i % 8
                total[i // 8] = total[i // 8] + roll(rows[i], 4 * slot - low, 1)
        packed.append(total)
    south, north = packed
    within = in_grid("gy")
    for j in range(4):
        even_ref[j] = jnp.where(par_y == 0, north[j], south[j])
        odd_ref[j] = jnp.where(within == 0, 0.0, jnp.where(par_y == 0, south[j], north[j]))


def one_hot(values, lanes):
    hit = index_of((CY, lanes), 0).astype(BF16) == values.astype(BF16)
    return jnp.where(hit, jnp.ones((), BF16), jnp.zeros((), BF16))


def split(x, parts):
    out = []
    for _ in range(parts):
        piece = x.astype(BF16)
        out.append(piece)
        x = x - piece.astype(F32)
    return out


def sample(tab_ref, cells, found_ref):
    lanes = cells.shape[1]
    hot = one_hot(cells & (CY - 1), lanes)
    hot = jnp.concatenate([(hot * jnp.asarray(STEP_DOWN**n, BF16)).astype(F8) for n in range(PARTS)], axis=0)
    found_ref[...] = jnp.dot(tab_ref[...], hot, preferred_element_type=F32)
    high = cells >> 8
    column = high & (CX - 1)
    west_row = jnp.where(column == 0, NZ * CX + (high >> 4), high - 1)
    here = jnp.broadcast_to(high >> 3, (8, lanes))
    beside = jnp.broadcast_to(west_row >> 3, (8, lanes))
    west = east = north = south = top = bottom = satur = jnp.zeros((8, lanes), F32)
    for g in range(22):
        at = 8 * g
        face = found_ref[at : at + 8, :]
        west = jnp.where(beside == g, face, west)
        if g < 20:
            mask = here == g
            east = jnp.where(mask, face, east)
            north = jnp.where(mask, found_ref[NORTH + at : NORTH + at + 8, :], north)
            south = jnp.where(mask, found_ref[SOUTH + at : SOUTH + at + 8, :], south)
            satur = jnp.where(mask, found_ref[SATUR + at : SATUR + at + 8, :], satur)
            if g < 18:
                top = jnp.where(mask, found_ref[LEVEL + at : LEVEL + at + 8, :], top)
            if g >= 2:
                bottom = jnp.where(mask, found_ref[LEVEL + at - 16 : LEVEL + at - 8, :], bottom)
    row = index_of((8, lanes), 0)
    own = row == (high & 7)
    other = row == (west_row & 7)

    def pick(mask, rows):
        return jnp.sum(jnp.where(mask, rows, 0.0), axis=0, keepdims=True)

    values = [(other, west), (own, east), (own, south), (own, north), (own, bottom), (own, top), (own, satur)]
    scales = [SIDE_SCALE] * 4 + [LEVEL_SCALE] * 2 + [SATUR_SCALE]
    return [pick(mask, v) * (1.0 / scale) for (mask, v), scale in zip(values, scales)]


def advance(record, sampled):
    west, east, south, north, bottom, top, satur = sampled
    scale = TIME_STEP / (POROSITY * satur)
    move_x = scale * (west + record[0:1] * (east - west))
    move_y = scale * (south + record[1:2] * (north - south))
    move_z = scale * (bottom + record[2:3] * (top - bottom))
    row = index_of(record.shape, 0)
    step = jnp.where(
        (row == 0) | (row == 6),
        move_x,
        jnp.where((row == 1) | (row == 7), move_y, jnp.where(row == 2, move_z, TIME_STEP)),
    )
    decayed = record * jnp.exp(-DECAY_RATE * TIME_STEP * satur)
    return jnp.where(row == 4, decayed, jnp.where(row == 5, satur, record + step))


def advance_group(tab_ref, cell_ref, rec_ref, found_ref, first, size, store):
    cells = jnp.concatenate([cell_ref[pl.ds(first + j, 1), :] for j in range(size)], axis=1)
    sampled = sample(tab_ref, cells, found_ref)
    for j in range(size):
        mine = [v[:, 128 * j : 128 * j + 128] for v in sampled]
        store(first + j, advance(rec_ref[first + j], mine))


def beside_lanes(tiles):
    lane = index_of(tiles[0].shape, 1)
    ahead = [roll(t, -1, 1) for t in tiles]
    back = [roll(t, 1, 1) for t in tiles]
    after = [jnp.where(lane == 127, ahead[(j + 1) % 3], ahead[j]) for j in range(3)]
    before = [jnp.where(lane == 0, back[(j + 2) % 3], back[j]) for j in range(3)]
    return after, before


def sweep_kernel(
    small_ref, p_ref, c_ref, s_ref, q_ref, rxe_ref, rxo_ref, rye_ref, ryo_ref, rec_ref, cell_ref,
    head_ref, tab_ref, kept, xe_ref, xo_ref, ye_ref, yo_ref,
    h0, h1, cond, wx, rhs, inv, wy, wy_back, wz, flat, found, sent, final, live_ref, sem,
):
    par_x, par_y = parities()
    edge = jnp.zeros((NZ, 3, 8, 128), F32)
    for ref in (h0, h1, cond, wx):
        ref[:, :, 0:8, :] = edge
        ref[:, :, 8 + ROWS : TALL, :] = edge
    east = jnp.where(par_x == 0, rxe_ref[...], rxo_ref[...])
    west = jnp.where(par_x == 0, rxo_ref[...], rxe_ref[...])
    north = [jnp.where(par_y == 0, rye_ref[j], ryo_ref[j]) for j in range(4)]
    south = [jnp.where(par_y == 0, ryo_ref[j], rye_ref[j]) for j in range(4)]
    lane = index_of((1, 128), 1)
    for f, (ref, base) in enumerate(((h0, 8), (cond, 8), (inv, 0), (rhs, 0))):
        for j in range(2):
            at = slice(128 * j, 128 * j + 128)
            own = (p_ref, c_ref, s_ref)[f][:, :, at] if f < 3 else s_ref[:, :, at] * p_ref[:, :, at] + q_ref[:, :, at]
            ref[:, j, base : base + 4, :] = west[:, 4 * f : 4 * f + 4, at]
            ref[:, j, base + 4 : base + 4 + CX, :] = own
            ref[:, j, base + 4 + CX : base + ROWS, :] = east[:, 4 * f : 4 * f + 4, at]
        for i in range(30):
            k, t = divmod(i, 3)
            slot = 8 * f + i % 8
            up = roll(north[i // 8], -4 * slot, 1)
            down = roll(south[i // 8], 124 - 4 * slot, 1)
            rows = jnp.where(lane < 4, up, jnp.where(lane >= 124, down, 0.0))
            if t < 2:
                ref[k, 2, base + 4 + 8 * t : base + 12 + 8 * t, :] = rows
            else:
                ref[k, 2, base + 4 + CX : base + ROWS, :] = rows[0:4]
                ref[k, 2, base : base + 4, :] = rows[4:8]
    for k in range(NZ):
        c = [cond[k, j, MID, :] for j in range(3)]
        after, _ = beside_lanes(c)
        w_y = [harmonic(c[j], after[j]) for j in range(3)]
        _, w_back = beside_lanes(w_y)
        for j in range(3):
            wx[k, j, MID, :] = harmonic(c[j], cond[k, j, 9 : 9 + ROWS, :])
            wy[k, j] = w_y[j]
            wy_back[k, j] = w_back[j]
            diag = inv[k, j] + wx[k, j, MID, :] + wx[k, j, 7 : 7 + ROWS, :] + w_y[j] + w_back[j]
            if k > 0:
                diag = diag + wz[k - 1, j]
            if k < NZ - 1:
                w_z = VERTICAL * harmonic(c[j], cond[k + 1, j, MID, :])
                wz[k, j] = w_z
                diag = diag + w_z
            inv[k, j] = OMEGA_RELAX / (diag + (diag == 0.0).astype(F32))
    old, new = h0, h1
    for _ in range(ITERS):
        for k in range(NZ):
            h = [old[k, j, MID, :] for j in range(3)]
            after, before = beside_lanes(h)
            for j in range(3):
                total = rhs[k, j]
                if k > 0:
                    total = total + wz[k - 1, j] * old[k - 1, j, MID, :]
                if k < NZ - 1:
                    total = total + wz[k, j] * old[k + 1, j, MID, :]
                along_x = wx[k, j, MID, :] * old[k, j, 9 : 9 + ROWS, :] + wx[k, j, 7 : 7 + ROWS, :] * old[k, j, 7 : 7 + ROWS, :]
                along_y = wy[k, j] * after[j] + wy_back[k, j] * before[j]
                new[k, j, MID, :] = (1.0 - OMEGA_RELAX) * h[j] + inv[k, j] * (along_x + along_y + total)
        old, new = new, old
    flat[NZ * CX : NORTH, :] = jnp.zeros((16, CY), F32)
    for k in range(NZ):
        h = [old[k, j, OWN, :] for j in range(3)]
        after, before = beside_lanes(h)
        at = slice(CX * k, CX * k + CX)
        for j in range(2):
            lanes = slice(128 * j, 128 * j + 128)

            def put(first, value):
                flat[first + CX * k : first + CX * k + CX, lanes] = value

            final[k, :, lanes] = h[j]
            put(EAST, -SIDE_SCALE * wx[k, j, OWN, :] * (old[k, j, 13 : 13 + CX, :] - h[j]))
            flat[NZ * CX + k : NZ * CX + k + 1, lanes] = -SIDE_SCALE * wx[k, j, 11:12, :] * (h[j][0:1] - old[k, j, 11:12, :])
            put(NORTH, -SIDE_SCALE * wy[k, j, INNER, :] * (after[j] - h[j]))
            put(SOUTH, -SIDE_SCALE * wy_back[k, j, INNER, :] * (h[j] - before[j]))
            if k < NZ - 1:
                put(LEVEL, -LEVEL_SCALE * wz[k, j, INNER, :] * (old[k + 1, j, OWN, :] - h[j] + 1.0))
            suction = jnp.maximum(-h[j], 0.0)
            put(SATUR, SATUR_SCALE * (RESIDUAL_SAT + (1.0 - RESIDUAL_SAT) * lax.rsqrt(1.0 + suction * suction)))
    head_copy = pltpu.make_async_copy(final, head_ref, sem)
    head_copy.start()
    rest = flat[...]
    for n in range(PARTS):
        piece = rest.astype(F8)
        tab_ref[:, CY * n : CY * n + CY] = piece
        rest = (rest - piece.astype(F32)) * (1.0 / STEP_DOWN)
    counts = small_ref[16:17, :]
    first = 0
    for d, cap in enumerate((CAPX, CAPX, CAPY, CAPY)):
        count = jnp.sum(jnp.where(lane == d, counts, 0), axis=1, keepdims=True)
        live_ref[first : first + cap, :] = (index_of((cap, 128), 0) < count).astype(F32)
        first += cap

    def store(slot, record):
        live = live_ref[pl.ds(slot, 1), :] > 0.0
        kept[slot] = jnp.where(live, 0.0, record)
        sent[slot] = jnp.where(live, record, 0.0)

    def group_step(i, carry):
        advance_group(tab_ref, cell_ref, rec_ref, found, i * GROUP_SENT, GROUP_SENT, store)
        return carry

    lax.fori_loop(0, SENT // GROUP_SENT, group_step, 0)
    links = jnp.concatenate([small_ref[j : j + 1, :] for j in range(8)], axis=1)
    surface = jnp.concatenate(split(final[NZ - 1], 3), axis=0)
    at_links = jnp.dot(surface, one_hot(links & (CY - 1), 1024), preferred_element_type=F32)
    at_links = at_links[0:CX] + at_links[CX : 2 * CX] + at_links[2 * CX : 3 * CX]
    picked = jnp.where(index_of((CX, 1024), 0) == (links >> 8), at_links, 0.0)
    value = jnp.sum(picked, axis=0, keepdims=True)
    flow = jnp.maximum(value, 0.0) + jnp.log1p(jnp.exp(-jnp.abs(value)))
    flows = [
        jnp.concatenate([flow[:, 256 * d : 256 * d + 128], flow[:, 256 * d + 128 : 256 * d + 256]] * 4, axis=0)
        for d in range(4)
    ]
    for ref, par, low, cap, within in (
        (xe_ref, par_x, 0, CAPX, None),
        (xo_ref, 1 - par_x, 0, CAPX, in_grid("gx")),
        (ye_ref, par_y, 2, CAPY, None),
        (yo_ref, 1 - par_y, 2, CAPY, in_grid("gy")),
    ):
        base = 2 * CAPX if low else 0
        leaving = sent[pl.ds(base + par * cap, cap)]
        flow_out = jnp.where(par == 0, flows[low], flows[low + 1])
        ref[0:cap] = leaving if within is None else jnp.where(within == 0, 0.0, leaving)
        ref[cap] = flow_out if within is None else jnp.where(within == 0, 0.0, flow_out)
    head_copy.wait()


def rest_kernel(first, size, tab_ref, rec_ref, cell_ref, small_ref, *refs):
    kept, hot_ref, found = refs[-3:]
    links = jnp.concatenate([small_ref[j : j + 1, :] for j in range(8, 16)], axis=1)
    hot_ref[...] = one_hot(links & (CY - 1), 1024)

    def store(slot, record):
        kept[slot - first] = record

    advance_group(tab_ref, cell_ref, rec_ref, found, first, size, store)


def arrive_kernel(small_ref, hot_ref, xe_ref, xo_ref, ye_ref, yo_ref, *refs):
    kept = refs[:-3]
    next_ref, inflow_ref, sems = refs[-3:]
    par_x, par_y = parities()
    copies = []

    def send(source, first, count):
        copy = pltpu.make_async_copy(source, next_ref.at[pl.ds(first, count)], sems.at[len(copies)])
        copy.start()
        copies.append(copy)

    send(kept[0], 0, SENT)
    first = SENT
    for ref, size in zip(kept[1:], GROUPS_KEEP):
        send(ref, first, size)
        first += size
    for ref, par, base, cap in (
        (xe_ref, 1 - par_x, PB, CAPX),
        (xo_ref, par_x, PB, CAPX),
        (ye_ref, 1 - par_y, PB + 2 * CAPX, CAPY),
        (yo_ref, par_y, PB + 2 * CAPX, CAPY),
    ):
        send(ref.at[pl.ds(0, cap)], base + par * cap, cap)
    x_even, x_odd = xe_ref[CAPX], xo_ref[CAPX]
    y_even, y_odd = ye_ref[CAPY], yo_ref[CAPY]
    arrivals = [
        jnp.where(par_x == 0, x_odd, x_even),
        jnp.where(par_x == 0, x_even, x_odd),
        jnp.where(par_y == 0, y_odd, y_even),
        jnp.where(par_y == 0, y_even, y_odd),
    ]
    flow = jnp.concatenate([a[r : r + 1] for a in arrivals for r in range(2)], axis=1)
    links = jnp.concatenate([small_ref[j : j + 1, :] for j in range(8, 16)], axis=1)
    spread = jnp.where(index_of((CX, 1024), 0) == (links >> 8), flow, 0.0)
    parts = jnp.concatenate(split(spread, 3), axis=0)
    total = lax.dot_general(parts, hot_ref[...], (((1,), (1,)), ((), ())), preferred_element_type=F32)
    inflow_ref[...] = total[0:CX] + total[CX : 2 * CX] + total[2 * CX : 3 * CX]
    for copy in copies:
        copy.wait()


VMEM = pl.BlockSpec(memory_space=pltpu.VMEM)
ANY = pl.BlockSpec(memory_space=pl.ANY)
LIMIT = pltpu.CompilerParams(vmem_limit_bytes=44 << 20)


AXES = ("gx", "gy")


def swap(value, axis, first):
    sizes = [lax.axis_size(name) for name in AXES]
    along, across = AXES.index(axis), 1 - AXES.index(axis)

    def place(i, other):
        at = (i, other) if along == 0 else (other, i)
        return at[0] * sizes[1] + at[1]

    pairs = []
    for other in range(sizes[across]):
        for i in range(first, sizes[along] - 1, 2):
            pairs.append((place(i, other), place(i + 1, other)))
    if first:
        for end in (0, sizes[along] - 1):
            for other in range(0, sizes[across], 2):
                pairs.append((place(end, other), place(end, other + 1)))
    return lax.ppermute(value, AXES, pairs + [(b, a) for a, b in pairs])


def exchange(even, odd, axis):
    from_odd = swap(odd, axis, 1)
    from_even = swap(even, axis, 0)
    return from_even, from_odd


def shape(*dims, dtype=F32):
    return jax.ShapeDtypeStruct(dims, dtype)


def body(
    pressure, conductivity, storage, source, particles, crossing, particle_cell, river_source, river_target
):
    counts = jnp.pad(crossing.reshape(1, 4), ((0, 7), (0, 124)))
    small = jnp.concatenate([river_source.reshape(8, 128), river_target.reshape(8, 128), counts], axis=0)
    grid = (pressure, conductivity, storage, source)
    tile = pltpu.VMEM((NZ, CX, CY), F32)
    x_odd, *grid = pl.pallas_call(
        odd_rows_kernel,
        out_shape=(shape(NZ, CX, CY),) * 5,
        in_specs=[ANY] * 4,
        out_specs=(VMEM,) * 5,
        scratch_shapes=[pltpu.SemaphoreType.DMA((2, 4))],
        compiler_params=pltpu.CompilerParams(vmem_limit_bytes=54400 << 10),
        name="odd_rows",
    )(*grid)
    from_odd = swap(x_odd, "gx", 1)
    x_even = pl.pallas_call(
        even_rows_kernel,
        out_shape=shape(NZ, CX, CY),
        in_specs=[VMEM] * 4,
        out_specs=VMEM,
        compiler_params=LIMIT,
        name="even_rows",
    )(*grid)
    halo_x = (swap(x_even, "gx", 0), from_odd)
    y_even, y_odd = pl.pallas_call(
        edge_lanes_kernel,
        out_shape=(shape(4, 8, 128), shape(4, 8, 128)),
        in_specs=[VMEM] * 6,
        out_specs=(VMEM, VMEM),
        compiler_params=LIMIT,
        name="edge_lanes",
    )(*grid, *halo_x)
    halo_y = exchange(y_even, y_odd, "gy")
    records = particles[0, 0]
    cells = particle_cell[0, 0]
    tall = pltpu.VMEM((NZ, 3, TALL, 128), F32)
    field = pltpu.VMEM((NZ, 3, ROWS, 128), F32)
    head, table, kept, x_even, x_odd, y_even, y_odd = pl.pallas_call(
        sweep_kernel,
        out_shape=(
            shape(NZ, CX, CY),
            shape(TABLE, PARTS * CY, dtype=F8),
            shape(SENT, 8, 128),
            shape(CAPX + 1, 8, 128),
            shape(CAPX + 1, 8, 128),
            shape(CAPY + 1, 8, 128),
            shape(CAPY + 1, 8, 128),
        ),
        in_specs=[VMEM] * 11,
        out_specs=(ANY,) + (VMEM,) * 6,
        scratch_shapes=[tall] * 4
        + [field] * 5
        + [
            pltpu.VMEM((TABLE, CY), F32),
            pltpu.VMEM((TABLE, 128 * GROUP_SENT), F32),
            pltpu.VMEM((SENT, 8, 128), F32),
            tile,
            pltpu.VMEM((SENT, 128), F32),
            pltpu.SemaphoreType.DMA,
        ],
        compiler_params=LIMIT,
        name="sweep",
    )(small, *grid, *halo_x, *halo_y, records, cells)
    stages = ((("x_odd", "gx", 1), ("y_even", "gy", 0), ("y_odd", "gy", 1), ("x_even", "gx", 0)),)
    waiting = {"x_odd": x_odd, "y_even": y_even, "y_odd": y_odd, "x_even": x_even}
    received = {}
    done = [kept]
    first = SENT
    for n, stage in enumerate(stages):
        for name, axis, parity in stage:
            received[name] = swap(waiting[name], axis, parity)
        later = [name for name, _, _ in stages[n + 1]] if n + 1 < len(stages) else []
        size = GROUPS_KEEP[n]
        outs = pl.pallas_call(
            functools.partial(rest_kernel, first, size),
            out_shape=[jax.ShapeDtypeStruct(waiting[v].shape, F32) for v in later] + [shape(size, 8, 128), shape(CY, 1024, dtype=BF16)],
            in_specs=[VMEM] * (4 + len(later)),
            out_specs=[VMEM] * (2 + len(later)),
            scratch_shapes=[pltpu.VMEM((TABLE, 128 * size), F32)],
            input_output_aliases={4 + i: i for i in range(len(later))},
            compiler_params=LIMIT,
            cost_estimate=pl.CostEstimate(
                flops=2 * TABLE * 512 * 128 * size, bytes_accessed=1 << 20, transcendentals=0
            ),
            name=f"rest_{n}",
        )(table, records, cells, small, *(waiting[v] for v in later))
        done.append(outs[-2])
        hot = outs[-1]
        waiting.update(zip(later, outs))
        first += size
    moved, inflow = pl.pallas_call(
        arrive_kernel,
        out_shape=(shape(OUT, 8, 128), shape(CX, CY)),
        in_specs=[VMEM] * (6 + len(done)),
        out_specs=(ANY, VMEM),
        scratch_shapes=[pltpu.SemaphoreType.DMA((4 + len(done),))],
        compiler_params=LIMIT,
        name="arrive",
    )(small, hot, *(received[v] for v in ("x_even", "x_odd", "y_even", "y_odd")), *done)
    return head, moved[None, None], inflow


def solution(mesh):
    in_specs = (
        P(None, "gx", "gy"),
        P(None, "gx", "gy"),
        P(None, "gx", "gy"),
        P(None, "gx", "gy"),
        P("gx", "gy", None, None, None),
        P("gx", "gy", None),
        P("gx", "gy", None, None),
        P("gx", "gy", None, None, None),
        P("gx", "gy", None, None, None),
    )
    out_specs = (P(None, "gx", "gy"), P("gx", "gy", None, None, None), P("gx", "gy"))
    return jax.shard_map(body, mesh=mesh, in_specs=in_specs, out_specs=out_specs, check_vma=False)
```
